32 devices in a mesh: row: 4 (over y, x), col: 8 (over z, core).
Axes of the slice: x: 2, y: 2, z: 4, core: 2. Of those that a mesh axis runs over, the one named last changes fastest.
Arguments:
- matrix: float32 [20480, 20480], P('row', 'col'), as said below
Outputs:
- factored: float32 [20480, 20480], P('row', 'col')
Inputs may be any that keep to these rules, and one draw needn't show every extreme that they name: `matrix`: symmetric positive definite in global order, stored in the tile storage of the statement.
All inputs are finite; a program needn't handle non-finite values.
Results may differ from the reference program's by a relative error of at most 0.000053.
Values sent between devices are 32-bit elements; how exact they have to be, the bound alone decides.
No kernel may reach another device: no remote copies, remote signals or barrier semaphores. Data moves between devices by JAX's collectives and lax.ppermute only.
A program may use at most 256 MiB of HBM per device.

```python
import jax
import jax.numpy as jnp
from jax import lax

TILE = 128
TILES = 160
ORDER = 20480
N_ROW = 4
N_COL = 8


def to_stored_draw(whole):
    rows_tiles = TILES // N_ROW
    cols_tiles = TILES // N_COL
    shaped = whole.reshape(rows_tiles, N_ROW, TILE, cols_tiles, N_COL, TILE)
    return shaped.transpose(1, 0, 2, 4, 3, 5).reshape(ORDER, ORDER)


def stokeslet_blocks(px_pos, py_pos, pz_pos, radius):
    delta_x = px_pos[:, None] - px_pos[None, :]
    delta_y = py_pos[:, None] - py_pos[None, :]
    delta_z = pz_pos[:, None] - pz_pos[None, :]
    dist_sq = delta_x * delta_x + delta_y * delta_y + delta_z * delta_z
    soft = dist_sq + radius
    factor = 0.5 / (soft * jnp.sqrt(soft))
    isotropic = (dist_sq + 2.0) * factor
    parts = (delta_x, delta_y, delta_z)
    rows_list = []
    for first in range(3):
        entries = []
        for second in range(3):
            entry = parts[first] * parts[second] * factor
            if first == second:
                entry = entry + isotropic
            entries.append(entry)
        rows_list.append(jnp.stack(entries, axis=-1))
    return jnp.stack(rows_list, axis=1)


def draw_matrix(key, part):
    key = jax.random.fold_in(key, 11)
    key_x, key_y, key_z, key_shift, key_scale = jax.random.split(key, 5)
    count = (ORDER + 2) // 3
    side = (2.0 * count) ** (1.0 / 3.0)
    height = 0.5 * side
    px_pos = jax.random.uniform(key_x, (count,), jnp.float32, 0.0, side)
    py_pos = jax.random.uniform(key_y, (count,), jnp.float32, 0.0, side)
    lift = jax.random.uniform(key_z, (count,), jnp.float32, 0.0, 1.0)
    pz_pos = height * lift
    radius = 1.0
    shift = jax.random.uniform(key_shift, (ORDER,), jnp.float32, 0.3, 1.0)
    scales = jnp.exp(jax.random.uniform(key_scale, (ORDER,), jnp.float32, -0.69, 0.69))
    blocks = stokeslet_blocks(px_pos, py_pos, pz_pos, radius)
    whole = blocks.reshape(3 * count, 3 * count)[:ORDER, :ORDER]
    index = jnp.arange(ORDER)
    whole = whole.at[index, index].add(shift)
    whole = whole * (scales[:, None] * scales[None, :])
    return to_stored_draw(whole)


def setup_inputs(seed: int = 0) -> dict:
    seeds = jax.random.split(jax.random.key(seed), 2)
    matrix = draw_matrix(jax.random.fold_in(seeds[1], 71), 0)
    return {"matrix": matrix}


def to_global(stored):
    rows_tiles = TILES // N_ROW
    cols_tiles = TILES // N_COL
    shaped = stored.reshape(N_ROW, rows_tiles, TILE, N_COL, cols_tiles, TILE)
    return shaped.transpose(1, 0, 2, 4, 3, 5).reshape(ORDER, ORDER)

def to_stored(whole):
    rows_tiles = TILES // N_ROW
    cols_tiles = TILES // N_COL
    shaped = whole.reshape(rows_tiles, N_ROW, TILE, cols_tiles, N_COL, TILE)
    return shaped.transpose(1, 0, 2, 4, 3, 5).reshape(ORDER, ORDER)

def product_t(left, right):
    return lax.dot_general(left.astype(jnp.float32), right.astype(jnp.float32), (((1,), (1,)), ((), ())), precision=lax.Precision.HIGHEST, preferred_element_type=jnp.float32)

def one_panel(square):
    lower = jnp.linalg.cholesky(square[:TILE, :TILE])
    identity = jnp.eye(TILE, dtype=lower.dtype)
    inverse = lax.linalg.triangular_solve(lower, identity, left_side=True, lower=True)
    solved = product_t(square[TILE:, :TILE], inverse)
    trailing = square[TILE:, TILE:] - product_t(solved, solved)
    return (jnp.concatenate([lower, solved], axis=0), trailing)

def reference(matrix):
    whole = to_global(matrix)
    first_col, schur_one = one_panel(whole)
    second_col, schur_two = one_panel(schur_one)
    result = jnp.zeros((ORDER, ORDER), jnp.float32)
    result = result.at[:, :TILE].set(first_col)
    result = result.at[TILE:, TILE:2 * TILE].set(second_col)
    result = result.at[2 * TILE:, 2 * TILE:].set(schur_two)
    return to_stored(result)
```

```python
import functools

import jax
import jax.numpy as jnp
from jax import lax
from jax.experimental import pallas as pl
from jax.experimental.pallas import tpu as pltpu
from jax.sharding import PartitionSpec as P

TILE = 128
PANELS = 2
WIDE = PANELS * TILE
CORES = 2
VMEM_LIMIT = 40 * 1024 * 1024
GROUP = 8


def dot_full(left, right, dims=((1,), (0,))):
    return lax.dot_general(
        left,
        right,
        (dims, ((), ())),
        precision=lax.Precision.HIGHEST,
        preferred_element_type=jnp.float32,
    )


def dot_half(left, right):
    return lax.dot_general(
        left, right, (((1,), (0,)), ((), ())), preferred_element_type=jnp.float32
    )


def split_half(value):
    high = value.astype(jnp.bfloat16)
    low = (value - high.astype(jnp.float32)).astype(jnp.bfloat16)
    return high, low


def factor_tile(square):
    groups = TILE // GROUP
    lane = lax.broadcasted_iota(jnp.int32, (GROUP, TILE), 1)
    sub = lax.broadcasted_iota(jnp.int32, (GROUP, TILE), 0)
    sub_col = lax.broadcasted_iota(jnp.int32, (GROUP, 1), 0)
    left = [square[g * GROUP : (g + 1) * GROUP] for g in range(groups)]
    right = [jnp.where(lane == sub + g * GROUP, 1.0, 0.0) for g in range(groups)]
    for step in range(TILE):
        group, place = divmod(step, GROUP)
        row_left = left[group][place : place + 1]
        row_right = right[group][place : place + 1]
        inverse = 1.0 / row_left[:, step : step + 1]
        row_left = row_left * inverse
        row_right = row_right * inverse
        for other in range(group, groups):
            column = left[other][:, step : step + 1]
            if other == group:
                column = jnp.where(sub_col > place, column, 0.0)
            left[other] = left[other] - column * row_left
            right[other] = right[other] - column * row_right
    upper, inverse = [], []
    for g in range(groups):
        row = sub + g * GROUP
        pivot = jnp.sum(jnp.where(lane == row, left[g], 0.0), axis=1, keepdims=True)
        scale = 1.0 / jnp.sqrt(pivot)
        upper.append(jnp.where(lane >= row, left[g] * scale, 0.0))
        inverse.append(right[g] * scale)
    return jnp.concatenate(upper, axis=0), jnp.concatenate(inverse, axis=0)


def corner_kernel(corner_ref, low_ref, inv_ref, inv_t_ref):
    zero = jnp.zeros((TILE, TILE), jnp.float32)
    upper_0, inv_0 = factor_tile(corner_ref[:TILE, :TILE])
    low_10 = dot_full(corner_ref[TILE:, :TILE], inv_0, ((1,), (1,)))
    square = corner_ref[TILE:, TILE:] - dot_full(low_10, low_10, ((1,), (1,)))
    upper_1, inv_1 = factor_tile(square)
    inv_10 = -dot_full(inv_1, dot_full(low_10, inv_0))
    low_ref[:TILE, :TILE] = upper_0.T
    low_ref[:TILE, TILE:] = zero
    low_ref[TILE:, :TILE] = low_10
    low_ref[TILE:, TILE:] = upper_1.T
    inv_ref[:TILE, :TILE] = inv_0
    inv_ref[:TILE, TILE:] = zero
    inv_ref[TILE:, :TILE] = inv_10
    inv_ref[TILE:, TILE:] = inv_1
    inv_t_ref[:TILE, :TILE] = inv_0.T
    inv_t_ref[:TILE, TILE:] = inv_10.T
    inv_t_ref[TILE:, :TILE] = zero
    inv_t_ref[TILE:, TILE:] = inv_1.T


def factor_corner(corner):
    shape = jax.ShapeDtypeStruct((WIDE, WIDE), jnp.float32)
    return pl.pallas_call(
        corner_kernel,
        out_shape=(shape, shape, shape),
        compiler_params=pltpu.CompilerParams(vmem_limit_bytes=VMEM_LIMIT),
        cost_estimate=pl.CostEstimate(flops=40_000_000, bytes_accessed=1 << 20, transcendentals=0),
    )(corner)


def columns_kernel(info_ref, inv_ref, *refs):
    parts = len(refs) // 2 - 1
    high_ref, low_ref = refs[-2:]
    odd = info_ref[0] % 2 == 1
    start = 0
    for part in range(parts):
        mine, other = refs[2 * part][...], refs[2 * part + 1][...]
        first = jnp.where(odd, other, mine)
        second = jnp.where(odd, mine, other)
        raw = jnp.concatenate([first, second], axis=0)
        size = raw.shape[1]
        high, low = split_half(dot_full(inv_ref[...], raw))
        high_ref[:, start : start + size] = high
        low_ref[:, start : start + size] = low
        start += size


def solve_columns(info, inverse, pairs):
    flat = [array for pair in pairs for array in pair]
    total = sum(pair[0].shape[1] for pair in pairs)
    shape = jax.ShapeDtypeStruct((WIDE, total), jnp.bfloat16)
    vmem = pl.BlockSpec(memory_space=pltpu.VMEM)
    return pl.pallas_call(
        columns_kernel,
        in_specs=[pl.BlockSpec(memory_space=pltpu.SMEM)] + [vmem] * (1 + len(flat)),
        out_specs=(vmem, vmem),
        out_shape=(shape, shape),
        compiler_params=pltpu.CompilerParams(vmem_limit_bytes=VMEM_LIMIT),
        cost_estimate=pl.CostEstimate(
            flops=12 * WIDE * WIDE * total, bytes_accessed=WIDE * total * 8, transcendentals=0
        ),
    )(info, inverse, *flat)


def update_kernel(chunk, depth, info_ref, mat_ref, high_ref, low_ref, lower_ref, inv_t_ref, *refs):
    mine_refs, other_refs = refs[:depth], refs[depth : 2 * depth]
    out_ref, raw, panel_high, panel_low, panel, sems = refs[-6:]
    row, place, core, col = info_ref[0], info_ref[1], info_ref[2], info_ref[3]
    step = pl.program_id(0)

    @pl.when(step == 0)
    def _():
        for source in range(depth):

            @pl.when(place == source)
            def _():
                mine_at = pl.ds(pl.multiple_of(core * TILE, TILE), TILE)
                other_at = pl.ds(pl.multiple_of((1 - core) * TILE, TILE), TILE)
                first = pltpu.make_async_copy(mine_refs[source], raw.at[:, mine_at], sems.at[0])
                second = pltpu.make_async_copy(other_refs[source], raw.at[:, other_at], sems.at[1])
                first.start()
                second.start()
                first.wait()
                second.wait()

        solved = dot_full(raw[...], inv_t_ref[...])
        if chunk == 0:
            head = jnp.where(row == 1, lower_ref[TILE:], solved[:TILE])
            head = jnp.where(row == 0, lower_ref[:TILE], head)
            solved = jnp.concatenate([head, solved[TILE:]], axis=0)
        high, low = split_half(solved)
        panel_high[...] = high
        panel_low[...] = low
        panel[...] = jnp.where(col == 1, solved[:, TILE:], solved[:, :TILE])

    high, low = panel_high[...], panel_low[...]
    right = high_ref[...]
    product = dot_half(high, right) + dot_half(low, right) + dot_half(high, low_ref[...])
    out_ref[...] = mat_ref[...] - product
    if chunk == 0:

        @pl.when(row < PANELS)
        def _():
            out_ref[:TILE, :] = jnp.zeros((TILE, out_ref.shape[1]), jnp.float32)

    @pl.when(jnp.logical_and(step == 0, col < PANELS))
    def _():
        out_ref[:, :TILE] = panel[...]


def update_chunk(chunk, rows, info, matrix, high, low, lower, inv_t, mine, other, out):
    depth = len(mine)
    columns = matrix.shape[1]
    block = next(b for b in (512, 640, 256, TILE) if columns % b == 0)
    any_spec = pl.BlockSpec(memory_space=pl.ANY)
    vmem = pl.BlockSpec(memory_space=pltpu.VMEM)
    window = pl.BlockSpec((rows, block), lambda j: (chunk, j))
    across = pl.BlockSpec((WIDE, block), lambda j: (0, j))
    in_specs = [pl.BlockSpec(memory_space=pltpu.SMEM), window, across, across, vmem, vmem]
    in_specs += [any_spec] * (2 * depth)
    operands = [info, matrix, high, low, lower, inv_t, *mine, *other]
    aliases = {}
    if out is not None:
        aliases = {len(operands): 0}
        in_specs.append(any_spec)
        operands.append(out)
    return pl.pallas_call(
        functools.partial(update_kernel, chunk, depth),
        grid=(columns // block,),
        in_specs=in_specs,
        out_specs=window,
        out_shape=jax.ShapeDtypeStruct(matrix.shape, jnp.float32),
        scratch_shapes=[
            pltpu.VMEM((rows, WIDE), jnp.float32),
            pltpu.VMEM((rows, WIDE), jnp.bfloat16),
            pltpu.VMEM((rows, WIDE), jnp.bfloat16),
            pltpu.VMEM((rows, TILE), jnp.float32),
            pltpu.SemaphoreType.DMA((2,)),
        ],
        input_output_aliases=aliases,
        compiler_params=pltpu.CompilerParams(vmem_limit_bytes=VMEM_LIMIT),
        cost_estimate=pl.CostEstimate(
            flops=6 * rows * columns * WIDE,
            bytes_accessed=8 * rows * columns,
            transcendentals=0,
        ),
    )(*operands)


def swap_pairs(count):
    return [(i, i ^ 1) for i in range(count)]


def share_corner(matrix, row, place, core, row_count, col_count):
    depth = col_count // CORES
    tile = matrix[:TILE, :TILE]
    beside = lax.ppermute(tile, "col", [(0, 1), (1, 0)])
    strip = jnp.concatenate(
        [jnp.where(core == 0, tile, beside), jnp.where(core == 0, beside, tile)], axis=1
    )
    got = [strip]
    for shift in range(1, row_count):
        pairs = [(p, (p + shift) % row_count) for p in range(PANELS)]
        got.append(lax.ppermute(strip, "row", pairs))
    strips = []
    for panel in range(PANELS):
        chosen = got[0]
        for shift in range(1, row_count):
            chosen = jnp.where((row - panel) % row_count == shift, got[shift], chosen)
        strips.append(chosen)
    square = jnp.concatenate(strips, axis=0)
    corner = square
    for shift in range(1, depth):
        pairs = [(c, c + CORES * shift) for c in range(CORES)]
        corner = jnp.where(place == shift, lax.ppermute(square, "col", pairs), corner)
    return corner


def share_rows(block, row, row_count):
    stride = PANELS
    while stride < row_count:
        pairs = [(i, i + stride) for i in range(min(stride, row_count - stride))]
        got = lax.ppermute(block, "row", pairs)
        block = jnp.where(jnp.logical_and(row >= stride, row < 2 * stride), got, block)
        stride *= 2
    return block, lax.ppermute(block, "row", swap_pairs(row_count))


def per_device(matrix):
    row_count = lax.axis_size("row")
    col_count = lax.axis_size("col")
    row = lax.axis_index("row")
    col = lax.axis_index("col")
    depth = col_count // CORES
    place, core = col // CORES, col % CORES
    info = jnp.stack([row, place, core, col]).astype(jnp.int32)
    row_tiles = matrix.shape[0] // TILE
    chunk_tiles = next(t for t in (5, 4, 2, 1) if row_tiles % t == 0 and row_tiles // t >= 5)
    rows = chunk_tiles * TILE
    chunks = row_tiles // chunk_tiles

    corner = share_corner(matrix, row, place, core, row_count, col_count)
    lower, inverse, inv_t = factor_corner(corner)

    half = matrix.shape[1] // 2
    pairs = [
        share_rows(matrix[:TILE, :half], row, row_count),
        share_rows(matrix[:TILE, half:], row, row_count),
    ]
    high, low = solve_columns(info, inverse, pairs)

    slots = chunks + depth - 1
    mine, other = [], []
    got = None
    for slot in range(slots):
        if slot < chunks:
            own = matrix[slot * rows : (slot + 1) * rows, :TILE]
            block = own if got is None else jnp.where(place == 0, own, got)
        else:
            block = got
        busy = [c for c in range(col_count) if 0 <= slot - c // CORES < chunks]
        mine.append(block)
        other.append(lax.ppermute(block, "col", [(c, c ^ 1) for c in busy]))
        hops = [(c, c + CORES) for c in busy if c + CORES < col_count]
        if hops:
            got = lax.ppermute(block, "col", hops)

    out = None
    for chunk in range(chunks):
        out = update_chunk(
            chunk,
            rows,
            info,
            matrix,
            high,
            low,
            lower,
            inv_t,
            mine[chunk : chunk + depth],
            other[chunk : chunk + depth],
            out,
        )
    return out


def solution(mesh):
    return jax.shard_map(
        per_device,
        mesh=mesh,
        in_specs=(P("row", "col"),),
        out_specs=P("row", "col"),
        check_vma=False,
    )
```

```python
import functools

import jax
import jax.numpy as jnp
from jax import lax
from jax.experimental import pallas as pl
from jax.experimental.pallas import tpu as pltpu
from jax.sharding import PartitionSpec as P

TILE = 128
PANELS = 2
WIDE = PANELS * TILE
CORES = 2
VMEM_LIMIT = 40 * 1024 * 1024
GROUP = 8
IN_SLOTS = 3
OUT_SLOTS = 2
PIECES = 4


def dot_full(left, right, dims=((1,), (0,))):
    return lax.dot_general(
        left,
        right,
        (dims, ((), ())),
        precision=lax.Precision.HIGHEST,
        preferred_element_type=jnp.float32,
    )


def dot_half(left, right):
    return lax.dot_general(
        left, right, (((1,), (0,)), ((), ())), preferred_element_type=jnp.float32
    )


def split_half(value):
    high = value.astype(jnp.bfloat16)
    low = (value - high.astype(jnp.float32)).astype(jnp.bfloat16)
    return high, low


def stack_halves(ref, value):
    high, low = split_half(value)
    ref[:WIDE] = high
    ref[WIDE : 2 * WIDE] = low
    ref[2 * WIDE :] = high


def spread_halves(value):
    high, low = split_half(value)
    return jnp.concatenate([high, high, low], axis=1)


def factor_tile(square):
    groups = TILE // GROUP
    shape = (GROUP, TILE)
    lane = lax.broadcasted_iota(jnp.int32, shape, 1)
    sub = lax.broadcasted_iota(jnp.int32, shape, 0)
    left = [square[g * GROUP : (g + 1) * GROUP] for g in range(groups)]
    right = [jnp.where(lane == sub + g * GROUP, 1.0, 0.0) for g in range(groups)]

    def row_of(value, index):
        return jnp.broadcast_to(value[index : index + 1], shape)

    def column_of(value, index):
        return jnp.broadcast_to(value[:, index : index + 1], shape)

    for g in range(groups):
        first = g * GROUP
        span = range(GROUP)
        columns = [column_of(left[g], first + b) for b in span]
        block = [[row_of(columns[b], a) if a <= b else None for b in span] for a in span]
        ratio = [[None] * GROUP for _ in span]
        inverse = []
        for s in span:
            inverse.append(1.0 / block[s][s])
            for t in range(s + 1, GROUP):
                ratio[t][s] = block[s][t] * inverse[s]
            for t in range(s + 1, GROUP):
                for b in range(t, GROUP):
                    block[t][b] = block[t][b] - ratio[t][s] * block[s][b]
        rows_left = [row_of(left[g], s) for s in span]
        rows_right = [row_of(right[g], s) for s in span]
        for t in span:
            for s in range(t):
                rows_left[t] = rows_left[t] - ratio[t][s] * rows_left[s]
                rows_right[t] = rows_right[t] - ratio[t][s] * rows_right[s]
        for s in span:
            left[g] = jnp.where(sub == s, rows_left[s], left[g])
            right[g] = jnp.where(sub == s, rows_right[s], right[g])
        rows_left = [rows_left[s] * inverse[s] for s in span]
        rows_right = [rows_right[s] * inverse[s] for s in span]
        for other in range(g + 1, groups):
            columns = [column_of(left[other], first + s) for s in span]
            for s in span:
                for t in range(s):
                    columns[s] = columns[s] - ratio[s][t] * columns[t]
            for s in span:
                left[other] = left[other] - columns[s] * rows_left[s]
                right[other] = right[other] - columns[s] * rows_right[s]
    upper, inverse = [], []
    for g in range(groups):
        row = sub + g * GROUP
        pivot = jnp.sum(jnp.where(lane == row, left[g], 0.0), axis=1, keepdims=True)
        scale = 1.0 / jnp.sqrt(pivot)
        upper.append(jnp.where(lane >= row, left[g] * scale, 0.0))
        inverse.append(right[g] * scale)
    return jnp.concatenate(upper, axis=0), jnp.concatenate(inverse, axis=0)


def corner_kernel(corner_ref, low_ref, inv_ref, inv_t_ref):
    zero = jnp.zeros((TILE, TILE), jnp.float32)
    upper_0, inv_0 = factor_tile(corner_ref[:TILE, :TILE])
    low_10 = dot_full(corner_ref[TILE:, :TILE], inv_0, ((1,), (1,)))
    square = corner_ref[TILE:, TILE:] - dot_full(low_10, low_10, ((1,), (1,)))
    upper_1, inv_1 = factor_tile(square)
    inv_10 = -dot_full(inv_1, dot_full(low_10, inv_0))
    low_ref[:TILE, :TILE] = upper_0.T
    low_ref[:TILE, TILE:] = zero
    low_ref[TILE:, :TILE] = low_10
    low_ref[TILE:, TILE:] = upper_1.T
    first = jnp.concatenate([inv_0, zero], axis=1)
    second = jnp.concatenate([inv_10, inv_1], axis=1)
    inv_ref[...] = spread_halves(jnp.concatenate([first, second], axis=0))
    first = jnp.concatenate([inv_0.T, inv_10.T], axis=1)
    second = jnp.concatenate([zero, inv_1.T], axis=1)
    stack_halves(inv_t_ref, jnp.concatenate([first, second], axis=0))


def factor_corner(corner):
    return pl.pallas_call(
        corner_kernel,
        out_shape=(
            jax.ShapeDtypeStruct((WIDE, WIDE), jnp.float32),
            jax.ShapeDtypeStruct((WIDE, 3 * WIDE), jnp.bfloat16),
            jax.ShapeDtypeStruct((3 * WIDE, WIDE), jnp.bfloat16),
        ),
        compiler_params=pltpu.CompilerParams(vmem_limit_bytes=VMEM_LIMIT),
        cost_estimate=pl.CostEstimate(flops=40_000_000, bytes_accessed=1 << 20, transcendentals=0),
    )(corner)


def columns_kernel(info_ref, inv_ref, *refs):
    out_ref, stack = refs[-2:]
    odd = info_ref[0] % 2 == 1
    start = 0
    for mine_ref, other_ref in zip(refs[0:-2:2], refs[1:-2:2]):
        size = mine_ref.shape[1]
        here = pl.ds(start, size)
        mine, other = mine_ref[...], other_ref[...]
        first = jnp.where(odd, other, mine)
        second = jnp.where(odd, mine, other)
        stack_halves(stack.at[:, here], jnp.concatenate([first, second], axis=0))
        stack_halves(out_ref.at[:, here], dot_half(inv_ref[...], stack[:, here]))
        start += size


def solve_columns(info, inverse, pairs):
    flat = [array for pair in pairs for array in pair]
    total = sum(pair[0].shape[1] for pair in pairs)
    vmem = pl.BlockSpec(memory_space=pltpu.VMEM)
    return pl.pallas_call(
        columns_kernel,
        in_specs=[pl.BlockSpec(memory_space=pltpu.SMEM)] + [vmem] * (1 + len(flat)),
        out_specs=vmem,
        out_shape=jax.ShapeDtypeStruct((3 * WIDE, total), jnp.bfloat16),
        scratch_shapes=[pltpu.VMEM((3 * WIDE, total), jnp.bfloat16)],
        compiler_params=pltpu.CompilerParams(vmem_limit_bytes=VMEM_LIMIT),
        cost_estimate=pl.CostEstimate(
            flops=6 * WIDE * WIDE * total, bytes_accessed=WIDE * total * 8, transcendentals=0
        ),
    )(info, inverse, *flat)


def update_kernel(
    start,
    rows,
    offset,
    strip,
    info_ref,
    mat_ref,
    right_ref,
    lower_ref,
    inv_t_ref,
    mine_ref,
    other_ref,
    *refs,
):
    out_ref, taken, given, panel, first_panel, in_sems, out_sems = refs[-7:]
    row, core, col = info_ref[0], info_ref[2], info_ref[3]
    columns = mat_ref.shape[1]
    steps = rows // strip
    block = next(b for b in (512, 640, 256, TILE) if columns % b == 0)
    piece = strip // PIECES

    def rows_at(ref, step, skip, count):
        return ref.at[pl.ds(pl.multiple_of(start + step * strip + skip, 8), count)]

    def take(step, slot):
        for p in range(PIECES):
            pltpu.make_async_copy(
                rows_at(mat_ref, step, p * piece, piece),
                taken.at[slot, pl.ds(p * piece, piece)],
                in_sems.at[slot],
            ).start()

    def give(step, slot):
        for p in range(PIECES):
            pltpu.make_async_copy(
                given.at[slot, pl.ds(p * piece, piece)],
                rows_at(out_ref, step, p * piece, piece),
                out_sems.at[slot],
            ).start()

    def wait_taken(step, slot):
        whole = rows_at(mat_ref, step, 0, strip)
        pltpu.make_async_copy(whole, taken.at[slot], in_sems.at[slot]).wait()

    def wait_given(step, slot):
        whole = rows_at(out_ref, step, 0, strip)
        pltpu.make_async_copy(given.at[slot], whole, out_sems.at[slot]).wait()

    for step in range(min(IN_SLOTS, steps)):
        take(step, step)

    @pl.loop(0, steps)
    def _(step):
        in_slot, out_slot = lax.rem(step, IN_SLOTS), lax.rem(step, OUT_SLOTS)
        here = pl.ds(pl.multiple_of(offset + step * strip, TILE), strip)
        mine, other = mine_ref[here], other_ref[here]
        raw = jnp.concatenate(
            [jnp.where(core == 1, other, mine), jnp.where(core == 1, mine, other)], axis=1
        )
        solved = dot_half(spread_halves(raw), inv_t_ref[...])
        panel[...] = spread_halves(solved)
        first_panel[...] = jnp.where(col == 1, solved[:, TILE:], solved[:, :TILE])
        top = jnp.logical_and(step == 0, row < PANELS)
        if start == 0:

            @pl.when(top)
            def _():
                head = jnp.where(row == 0, lower_ref[:TILE], lower_ref[TILE:])
                panel[:TILE] = spread_halves(head)
                first_panel[:TILE] = jnp.where(col == 1, head[:, TILE:], head[:, :TILE])

        wait_taken(step, in_slot)

        @pl.when(step >= OUT_SLOTS)
        def _():
            wait_given(step - OUT_SLOTS, out_slot)

        @pl.loop(0, columns // block)
        def _(index):
            across = pl.ds(pl.multiple_of(index * block, block), block)
            product = dot_half(panel[...], right_ref[:, across])
            given[out_slot, :, across] = taken[in_slot, :, across] - product

        if start == 0:

            @pl.when(top)
            def _():
                given[out_slot, :TILE] = jnp.zeros((TILE, columns), jnp.float32)

        @pl.when(col < PANELS)
        def _():
            given[out_slot, :, :TILE] = first_panel[...]

        give(step, out_slot)

        @pl.when(step + IN_SLOTS < steps)
        def _():
            take(step + IN_SLOTS, in_slot)

    for step in range(max(steps - OUT_SLOTS, 0), steps):
        wait_given(step, step % OUT_SLOTS)


def update_rows(start, end, base, info, matrix, right, lower, inv_t, mine, other, out):
    rows, columns = end - start, matrix.shape[1]
    strip = 2 * TILE if rows % (2 * TILE) == 0 else TILE
    any_spec = pl.BlockSpec(memory_space=pl.ANY)
    vmem = pl.BlockSpec(memory_space=pltpu.VMEM)
    in_specs = [pl.BlockSpec(memory_space=pltpu.SMEM), any_spec] + [vmem] * 5
    operands = [info, matrix, right, lower, inv_t, mine, other]
    aliases = {}
    if out is not None:
        aliases = {len(operands): 0}
        in_specs.append(any_spec)
        operands.append(out)
    return pl.pallas_call(
        functools.partial(update_kernel, start, rows, start - base, strip),
        in_specs=in_specs,
        out_specs=any_spec,
        out_shape=jax.ShapeDtypeStruct(matrix.shape, jnp.float32),
        scratch_shapes=[
            pltpu.VMEM((IN_SLOTS, strip, columns), jnp.float32),
            pltpu.VMEM((OUT_SLOTS, strip, columns), jnp.float32),
            pltpu.VMEM((strip, 3 * WIDE), jnp.bfloat16),
            pltpu.VMEM((strip, TILE), jnp.float32),
            pltpu.SemaphoreType.DMA((IN_SLOTS,)),
            pltpu.SemaphoreType.DMA((OUT_SLOTS,)),
        ],
        input_output_aliases=aliases,
        compiler_params=pltpu.CompilerParams(vmem_limit_bytes=VMEM_LIMIT),
        cost_estimate=pl.CostEstimate(
            flops=6 * rows * columns * WIDE,
            bytes_accessed=8 * rows * columns,
            transcendentals=0,
        ),
    )(*operands)


def after(value, *earlier):
    return lax.optimization_barrier((value, *earlier))[0]


def double_rows(block, row, row_count):
    stride = PANELS
    while stride < row_count:
        pairs = [(i, i + stride) for i in range(min(stride, row_count - stride))]
        got = lax.ppermute(block, "row", pairs)
        block = jnp.where(jnp.logical_and(row >= stride, row < 2 * stride), got, block)
        stride *= 2
    return block


def swap_rows(block, row_count):
    return lax.ppermute(block, "row", [(i, i ^ 1) for i in range(row_count)])


def pick(blocks, index):
    chosen = blocks[0]
    for shift in range(1, len(blocks)):
        chosen = jnp.where(index == shift, blocks[shift], chosen)
    return chosen


def share_corner(matrix, row, place, core, row_count, col_count):
    depth = col_count // CORES
    tile = matrix[:TILE, :TILE]
    got = [tile]
    for shift in range(1, row_count):
        pairs = [
            (p * col_count + c, (p + shift) % row_count * col_count + c)
            for p in range(PANELS)
            for c in range(CORES)
        ]
        got.append(lax.ppermute(tile, ("row", "col"), pairs))
    column = jnp.concatenate([pick(got, (row - p) % row_count) for p in range(PANELS)], axis=0)
    beside = lax.ppermute(column, "col", [(0, 1), (1, 0)])
    square = jnp.concatenate(
        [jnp.where(core == 0, column, beside), jnp.where(core == 0, beside, column)], axis=1
    )
    got = [square]
    for shift in range(1, depth):
        pairs = [(c, c + CORES * shift) for c in range(CORES)]
        got.append(lax.ppermute(square, "col", pairs))
    return pick(got, place)


def spread_columns(block, place, col_count, between):
    stride = col_count // CORES // 2
    levels = []
    while stride > 0:
        block = after(block, *between[len(levels)])
        pairs = [(c, c + CORES * stride) for c in range(col_count) if c // CORES % (2 * stride) == 0]
        got = lax.ppermute(block, "col", pairs)
        block = jnp.where(place % (2 * stride) == stride, got, block)
        levels.append(block)
        stride //= 2
    return levels


def per_device(matrix):
    row_count = lax.axis_size("row")
    col_count = lax.axis_size("col")
    row = lax.axis_index("row")
    col = lax.axis_index("col")
    place, core = col // CORES, col % CORES
    info = jnp.stack([row, place, core, col]).astype(jnp.int32)
    tiles = matrix.shape[0] // TILE
    cut = tiles // 4 * 2 * TILE
    half = matrix.shape[1] // 2

    bands = [matrix[:TILE, :half], matrix[:TILE, half:]]
    bands = [double_rows(band, row, row_count) for band in bands]
    corner = share_corner(matrix, row, place, core, row_count, col_count)
    between = [()] + [(corner,)] * col_count
    first = spread_columns(matrix[:cut, :TILE], place, col_count, between)
    besides = [swap_rows(band, row_count) for band in bands]
    lower, inverse, inv_t = factor_corner(after(corner, besides[0], bands[1]))
    between = [(first[0],)] + [(inverse, besides[1])] * col_count
    second = spread_columns(matrix[cut:, :TILE], place, col_count, between)
    right = solve_columns(info, inverse, list(zip(bands, besides)))

    swap = [(c, c ^ 1) for c in range(col_count)]
    mine = first[-1]
    other = after(lax.ppermute(mine, "col", swap), *second[:-1])
    early = tiles // 8 * TILE
    shared = (info, matrix, right, lower, inv_t)
    out = update_rows(0, early, 0, *shared, mine, other, None)
    late_mine = second[-1]
    late_other = lax.ppermute(after(late_mine, out), "col", swap)
    out = update_rows(early, cut, 0, *shared, mine, other, out)
    return update_rows(cut, tiles * TILE, cut, *shared, late_mine, late_other, out)


def solution(mesh):
    return jax.shard_map(
        per_device,
        mesh=mesh,
        in_specs=(P("row", "col"),),
        out_specs=P("row", "col"),
        check_vma=False,
    )
```

```python
import functools

import jax
import jax.numpy as jnp
from jax import lax
from jax.experimental import pallas as pl
from jax.experimental.pallas import tpu as pltpu
from jax.sharding import PartitionSpec as P

TILE = 128
PANELS = 2
WIDE = PANELS * TILE
CORES = 2
VMEM_LIMIT = 40 * 1024 * 1024
GROUP = 8
IN_SLOTS = 3
OUT_SLOTS = 2
PIECES = 4


def dot_full(left, right, dims=((1,), (0,))):
    return lax.dot_general(
        left,
        right,
        (dims, ((), ())),
        precision=lax.Precision.HIGHEST,
        preferred_element_type=jnp.float32,
    )


def dot_half(left, right):
    return lax.dot_general(
        left, right, (((1,), (0,)), ((), ())), preferred_element_type=jnp.float32
    )


def split_half(value):
    high = value.astype(jnp.bfloat16)
    low = (value - high.astype(jnp.float32)).astype(jnp.bfloat16)
    return high, low


def stack_halves(ref, value):
    high, low = split_half(value)
    ref[:WIDE] = high
    ref[WIDE : 2 * WIDE] = low
    ref[2 * WIDE :] = high


def spread_halves(value):
    high, low = split_half(value)
    return jnp.concatenate([high, high, low], axis=1)


def factor_tile(square):
    groups = TILE // GROUP
    shape = (GROUP, TILE)
    lane = lax.broadcasted_iota(jnp.int32, shape, 1)
    sub = lax.broadcasted_iota(jnp.int32, shape, 0)
    left = [square[g * GROUP : (g + 1) * GROUP] for g in range(groups)]
    right = [jnp.where(lane == sub + g * GROUP, 1.0, 0.0) for g in range(groups)]

    def row_of(value, index):
        return jnp.broadcast_to(value[index : index + 1], shape)

    def column_of(value, index):
        return jnp.broadcast_to(value[:, index : index + 1], shape)

    for g in range(groups):
        first = g * GROUP
        span = range(GROUP)
        columns = [column_of(left[g], first + b) for b in span]
        block = [[row_of(columns[b], a) if a <= b else None for b in span] for a in span]
        ratio = [[None] * GROUP for _ in span]
        inverse = []
        for s in span:
            inverse.append(1.0 / block[s][s])
            for t in range(s + 1, GROUP):
                ratio[t][s] = block[s][t] * inverse[s]
            for t in range(s + 1, GROUP):
                for b in range(t, GROUP):
                    block[t][b] = block[t][b] - ratio[t][s] * block[s][b]
        rows_left = [row_of(left[g], s) for s in span]
        rows_right = [row_of(right[g], s) for s in span]
        for t in span:
            for s in range(t):
                rows_left[t] = rows_left[t] - ratio[t][s] * rows_left[s]
                rows_right[t] = rows_right[t] - ratio[t][s] * rows_right[s]
        for s in span:
            left[g] = jnp.where(sub == s, rows_left[s], left[g])
            right[g] = jnp.where(sub == s, rows_right[s], right[g])
        rows_left = [rows_left[s] * inverse[s] for s in span]
        rows_right = [rows_right[s] * inverse[s] for s in span]
        for other in range(g + 1, groups):
            columns = [column_of(left[other], first + s) for s in span]
            for s in span:
                for t in range(s):
                    columns[s] = columns[s] - ratio[s][t] * columns[t]
            for s in span:
                left[other] = left[other] - columns[s] * rows_left[s]
                right[other] = right[other] - columns[s] * rows_right[s]
    upper, inverse = [], []
    for g in range(groups):
        row = sub + g * GROUP
        pivot = jnp.sum(jnp.where(lane == row, left[g], 0.0), axis=1, keepdims=True)
        scale = 1.0 / jnp.sqrt(pivot)
        upper.append(jnp.where(lane >= row, left[g] * scale, 0.0))
        inverse.append(right[g] * scale)
    return jnp.concatenate(upper, axis=0), jnp.concatenate(inverse, axis=0)


def corner_kernel(corner_ref, low_ref, inv_ref, inv_t_ref):
    zero = jnp.zeros((TILE, TILE), jnp.float32)
    upper_0, inv_0 = factor_tile(corner_ref[:TILE, :TILE])
    low_10 = dot_full(corner_ref[TILE:, :TILE], inv_0, ((1,), (1,)))
    square = corner_ref[TILE:, TILE:] - dot_full(low_10, low_10, ((1,), (1,)))
    upper_1, inv_1 = factor_tile(square)
    inv_10 = -dot_full(inv_1, dot_full(low_10, inv_0))
    low_ref[:TILE, :TILE] = upper_0.T
    low_ref[:TILE, TILE:] = zero
    low_ref[TILE:, :TILE] = low_10
    low_ref[TILE:, TILE:] = upper_1.T
    first = jnp.concatenate([inv_0, zero], axis=1)
    second = jnp.concatenate([inv_10, inv_1], axis=1)
    inv_ref[...] = spread_halves(jnp.concatenate([first, second], axis=0))
    first = jnp.concatenate([inv_0.T, inv_10.T], axis=1)
    second = jnp.concatenate([zero, inv_1.T], axis=1)
    stack_halves(inv_t_ref, jnp.concatenate([first, second], axis=0))


def factor_corner(corner):
    return pl.pallas_call(
        corner_kernel,
        out_shape=(
            jax.ShapeDtypeStruct((WIDE, WIDE), jnp.float32),
            jax.ShapeDtypeStruct((WIDE, 3 * WIDE), jnp.bfloat16),
            jax.ShapeDtypeStruct((3 * WIDE, WIDE), jnp.bfloat16),
        ),
        compiler_params=pltpu.CompilerParams(vmem_limit_bytes=VMEM_LIMIT),
        cost_estimate=pl.CostEstimate(flops=40_000_000, bytes_accessed=1 << 20, transcendentals=0),
    )(corner)


def columns_kernel(info_ref, inv_ref, *refs):
    out_ref, stack = refs[-2:]
    odd = info_ref[0] % 2 == 1
    start = 0
    for mine_ref, other_ref in zip(refs[0:-2:2], refs[1:-2:2]):
        size = mine_ref.shape[1]
        here = pl.ds(start, size)
        mine, other = mine_ref[...], other_ref[...]
        first = jnp.where(odd, other, mine)
        second = jnp.where(odd, mine, other)
        stack_halves(stack.at[:, here], jnp.concatenate([first, second], axis=0))
        stack_halves(out_ref.at[:, here], dot_half(inv_ref[...], stack[:, here]))
        start += size


def solve_columns(info, inverse, pairs):
    flat = [array for pair in pairs for array in pair]
    total = sum(pair[0].shape[1] for pair in pairs)
    vmem = pl.BlockSpec(memory_space=pltpu.VMEM)
    return pl.pallas_call(
        columns_kernel,
        in_specs=[pl.BlockSpec(memory_space=pltpu.SMEM)] + [vmem] * (1 + len(flat)),
        out_specs=vmem,
        out_shape=jax.ShapeDtypeStruct((3 * WIDE, total), jnp.bfloat16),
        scratch_shapes=[pltpu.VMEM((3 * WIDE, total), jnp.bfloat16)],
        compiler_params=pltpu.CompilerParams(vmem_limit_bytes=VMEM_LIMIT),
        cost_estimate=pl.CostEstimate(
            flops=6 * WIDE * WIDE * total, bytes_accessed=WIDE * total * 8, transcendentals=0
        ),
    )(info, inverse, *flat)


def update_kernel(
    start,
    rows,
    offset,
    strip,
    info_ref,
    mat_ref,
    right_ref,
    lower_ref,
    inv_t_ref,
    mine_ref,
    other_ref,
    *refs,
):
    out_ref, taken, given, panel, first_panel, in_sems, out_sems = refs[-7:]
    row, core, col = info_ref[0], info_ref[2], info_ref[3]
    columns = mat_ref.shape[1]
    steps = rows // strip
    block = next(b for b in (512, 640, 256, TILE) if columns % b == 0)
    piece = strip // PIECES

    def rows_at(ref, step, skip, count):
        return ref.at[pl.ds(pl.multiple_of(start + step * strip + skip, 8), count)]

    def take(step, slot):
        for p in range(PIECES):
            pltpu.make_async_copy(
                rows_at(mat_ref, step, p * piece, piece),
                taken.at[slot, pl.ds(p * piece, piece)],
                in_sems.at[slot],
            ).start()

    def give(step, slot):
        for p in range(PIECES):
            pltpu.make_async_copy(
                given.at[slot, pl.ds(p * piece, piece)],
                rows_at(out_ref, step, p * piece, piece),
                out_sems.at[slot],
            ).start()

    def wait_taken(step, slot):
        whole = rows_at(mat_ref, step, 0, strip)
        pltpu.make_async_copy(whole, taken.at[slot], in_sems.at[slot]).wait()

    def wait_given(step, slot):
        whole = rows_at(out_ref, step, 0, strip)
        pltpu.make_async_copy(given.at[slot], whole, out_sems.at[slot]).wait()

    for step in range(min(IN_SLOTS, steps)):
        take(step, step)

    @pl.loop(0, steps)
    def _(step):
        in_slot, out_slot = lax.rem(step, IN_SLOTS), lax.rem(step, OUT_SLOTS)
        here = pl.ds(pl.multiple_of(offset + step * strip, TILE), strip)
        mine, other = mine_ref[here], other_ref[here]
        raw = jnp.concatenate(
            [jnp.where(core == 1, other, mine), jnp.where(core == 1, mine, other)], axis=1
        )
        solved = dot_half(spread_halves(raw), inv_t_ref[...])
        panel[...] = spread_halves(solved)
        first_panel[...] = jnp.where(col == 1, solved[:, TILE:], solved[:, :TILE])
        top = jnp.logical_and(step == 0, row < PANELS)
        if start == 0:

            @pl.when(top)
            def _():
                head = jnp.where(row == 0, lower_ref[:TILE], lower_ref[TILE:])
                panel[:TILE] = spread_halves(head)
                first_panel[:TILE] = jnp.where(col == 1, head[:, TILE:], head[:, :TILE])

        wait_taken(step, in_slot)

        @pl.when(step >= OUT_SLOTS)
        def _():
            wait_given(step - OUT_SLOTS, out_slot)

        @pl.loop(0, columns // block)
        def _(index):
            across = pl.ds(pl.multiple_of(index * block, block), block)
            product = dot_half(panel[...], right_ref[:, across])
            given[out_slot, :, across] = taken[in_slot, :, across] - product

        if start == 0:

            @pl.when(top)
            def _():
                given[out_slot, :TILE] = jnp.zeros((TILE, columns), jnp.float32)

        @pl.when(col < PANELS)
        def _():
            given[out_slot, :, :TILE] = first_panel[...]

        give(step, out_slot)

        @pl.when(step + IN_SLOTS < steps)
        def _():
            take(step + IN_SLOTS, in_slot)

    for step in range(max(steps - OUT_SLOTS, 0), steps):
        wait_given(step, step % OUT_SLOTS)


def update_rows(start, end, base, info, matrix, right, lower, inv_t, mine, other, out):
    rows, columns = end - start, matrix.shape[1]
    strip = 2 * TILE if rows % (2 * TILE) == 0 else TILE
    any_spec = pl.BlockSpec(memory_space=pl.ANY)
    vmem = pl.BlockSpec(memory_space=pltpu.VMEM)
    in_specs = [pl.BlockSpec(memory_space=pltpu.SMEM), any_spec] + [vmem] * 5
    operands = [info, matrix, right, lower, inv_t, mine, other]
    aliases = {}
    if out is not None:
        aliases = {len(operands): 0}
        in_specs.append(any_spec)
        operands.append(out)
    return pl.pallas_call(
        functools.partial(update_kernel, start, rows, start - base, strip),
        in_specs=in_specs,
        out_specs=any_spec,
        out_shape=jax.ShapeDtypeStruct(matrix.shape, jnp.float32),
        scratch_shapes=[
            pltpu.VMEM((IN_SLOTS, strip, columns), jnp.float32),
            pltpu.VMEM((OUT_SLOTS, strip, columns), jnp.float32),
            pltpu.VMEM((strip, 3 * WIDE), jnp.bfloat16),
            pltpu.VMEM((strip, TILE), jnp.float32),
            pltpu.SemaphoreType.DMA((IN_SLOTS,)),
            pltpu.SemaphoreType.DMA((OUT_SLOTS,)),
        ],
        input_output_aliases=aliases,
        compiler_params=pltpu.CompilerParams(vmem_limit_bytes=VMEM_LIMIT),
        cost_estimate=pl.CostEstimate(
            flops=6 * rows * columns * WIDE,
            bytes_accessed=8 * rows * columns,
            transcendentals=0,
        ),
    )(*operands)


def after(value, *earlier):
    return lax.optimization_barrier((value, *earlier))[0]


def double_rows(block, row, row_count):
    stride = PANELS
    while stride < row_count:
        pairs = [(i, i + stride) for i in range(min(stride, row_count - stride))]
        got = lax.ppermute(block, "row", pairs)
        block = jnp.where(jnp.logical_and(row >= stride, row < 2 * stride), got, block)
        stride *= 2
    return block


def swap_rows(block, row_count):
    return lax.ppermute(block, "row", [(i, i ^ 1) for i in range(row_count)])


def pick(blocks, index):
    chosen = blocks[0]
    for shift in range(1, len(blocks)):
        chosen = jnp.where(index == shift, blocks[shift], chosen)
    return chosen


def share_corner(matrix, row, place, core, row_count, col_count):
    depth = col_count // CORES
    tile = matrix[:TILE, :TILE]
    got = [tile]
    for shift in range(1, row_count):
        pairs = [
            (p * col_count + c, (p + shift) % row_count * col_count + c)
            for p in range(PANELS)
            for c in range(CORES)
        ]
        got.append(lax.ppermute(tile, ("row", "col"), pairs))
    column = jnp.concatenate([pick(got, (row - p) % row_count) for p in range(PANELS)], axis=0)
    beside = lax.ppermute(column, "col", [(0, 1), (1, 0)])
    square = jnp.concatenate(
        [jnp.where(core == 0, column, beside), jnp.where(core == 0, beside, column)], axis=1
    )
    got = [square]
    for shift in range(1, depth):
        pairs = [(c, c + CORES * shift) for c in range(CORES)]
        got.append(lax.ppermute(square, "col", pairs))
    return column, pick(got, place)


def per_device(matrix):
    row_count = lax.axis_size("row")
    col_count = lax.axis_size("col")
    row = lax.axis_index("row")
    col = lax.axis_index("col")
    depth = col_count // CORES
    place, core = col // CORES, col % CORES
    info = jnp.stack([row, place, core, col]).astype(jnp.int32)
    tiles = matrix.shape[0] // TILE
    chunks = next(n for n in (5, 4, 2, 1) if tiles % n == 0)
    rows = tiles // chunks * TILE
    half = matrix.shape[1] // 2

    column, corner = share_corner(matrix, row, place, core, row_count, col_count)
    bands = [after(matrix[:TILE, :half], column), after(matrix[:TILE, half:], column)]
    bands = [double_rows(band, row, row_count) for band in bands]

    last = chunks + depth - 2
    held, got = [], None

    def fill(slot, *earlier):
        if slot < chunks:
            own = matrix[slot * rows : (slot + 1) * rows, :TILE]
            block = own if got is None else jnp.where(place == 0, own, got)
        else:
            block = got
        block = after(block, *earlier)
        held.append(block)
        if slot == last:
            return None
        busy = [c for c in range(col_count) if 0 <= slot - c // CORES < chunks]
        hops = [(c, c + CORES) for c in busy if c + CORES < col_count]
        return lax.ppermute(block, "col", hops)

    got = fill(0)
    got = fill(1, corner)
    got = fill(2, bands[0])
    lower, inverse, inv_t = factor_corner(after(corner, held[2]))
    besides = [swap_rows(band, row_count) for band in bands]
    slot = 3
    while slot < depth:
        got = fill(slot, inverse, bands[1], besides[0])
        slot += 1
    right = None
    out = None
    for chunk in range(chunks):
        mine = pick(held[chunk : chunk + depth], place)
        other = lax.ppermute(mine, "col", [(c, c ^ 1) for c in range(col_count)])
        if slot <= last:
            got = fill(slot) if out is None else fill(slot, out)
            slot += 1
        if right is None:
            right = solve_columns(info, inverse, list(zip(bands, besides)))
        other = after(other, held[-1])
        first = chunk * rows
        out = update_rows(
            first, first + rows, first, info, matrix, right, lower, inv_t, mine, other, out
        )
    return out


def solution(mesh):
    return jax.shard_map(
        per_device,
        mesh=mesh,
        in_specs=(P("row", "col"),),
        out_specs=P("row", "col"),
        check_vma=False,
    )
```

```python
import functools

import jax
import jax.numpy as jnp
from jax import lax
from jax.experimental import pallas as pl
from jax.experimental.pallas import tpu as pltpu
from jax.sharding import PartitionSpec as P

TILE = 128
PANELS = 2
WIDE = PANELS * TILE
CORES = 2
VMEM_LIMIT = 40 * 1024 * 1024
GROUP = 8
IN_SLOTS = 3
OUT_SLOTS = 2
PIECES = 4


def dot_full(left, right, dims=((1,), (0,))):
    return lax.dot_general(
        left,
        right,
        (dims, ((), ())),
        precision=lax.Precision.HIGHEST,
        preferred_element_type=jnp.float32,
    )


def dot_half(left, right):
    return lax.dot_general(
        left, right, (((1,), (0,)), ((), ())), preferred_element_type=jnp.float32
    )


def split_half(value):
    high = value.astype(jnp.bfloat16)
    low = (value - high.astype(jnp.float32)).astype(jnp.bfloat16)
    return high, low


def stack_halves(ref, value):
    high, low = split_half(value)
    ref[:WIDE] = high
    ref[WIDE : 2 * WIDE] = low
    ref[2 * WIDE :] = high


def spread_halves(value):
    high, low = split_half(value)
    return jnp.concatenate([high, high, low], axis=1)


def factor_tile(square):
    groups = TILE // GROUP
    shape = (GROUP, TILE)
    lane = lax.broadcasted_iota(jnp.int32, shape, 1)
    sub = lax.broadcasted_iota(jnp.int32, shape, 0)
    left = [square[g * GROUP : (g + 1) * GROUP] for g in range(groups)]
    right = [jnp.where(lane == sub + g * GROUP, 1.0, 0.0) for g in range(groups)]

    def row_of(value, index):
        return jnp.broadcast_to(value[index : index + 1], shape)

    def column_of(value, index):
        return jnp.broadcast_to(value[:, index : index + 1], shape)

    for g in range(groups):
        first = g * GROUP
        span = range(GROUP)
        columns = [column_of(left[g], first + b) for b in span]
        block = [[row_of(columns[b], a) if a <= b else None for b in span] for a in span]
        ratio = [[None] * GROUP for _ in span]
        inverse = []
        for s in span:
            inverse.append(1.0 / block[s][s])
            for t in range(s + 1, GROUP):
                ratio[t][s] = block[s][t] * inverse[s]
            for t in range(s + 1, GROUP):
                for b in range(t, GROUP):
                    block[t][b] = block[t][b] - ratio[t][s] * block[s][b]
        rows_left = [row_of(left[g], s) for s in span]
        rows_right = [row_of(right[g], s) for s in span]
        for t in span:
            for s in range(t):
                rows_left[t] = rows_left[t] - ratio[t][s] * rows_left[s]
                rows_right[t] = rows_right[t] - ratio[t][s] * rows_right[s]
        for s in span:
            left[g] = jnp.where(sub == s, rows_left[s], left[g])
            right[g] = jnp.where(sub == s, rows_right[s], right[g])
        rows_left = [rows_left[s] * inverse[s] for s in span]
        rows_right = [rows_right[s] * inverse[s] for s in span]
        for other in range(g + 1, groups):
            columns = [column_of(left[other], first + s) for s in span]
            for s in span:
                for t in range(s):
                    columns[s] = columns[s] - ratio[s][t] * columns[t]
            for s in span:
                left[other] = left[other] - columns[s] * rows_left[s]
                right[other] = right[other] - columns[s] * rows_right[s]
    upper, inverse = [], []
    for g in range(groups):
        row = sub + g * GROUP
        pivot = jnp.sum(jnp.where(lane == row, left[g], 0.0), axis=1, keepdims=True)
        scale = 1.0 / jnp.sqrt(pivot)
        upper.append(jnp.where(lane >= row, left[g] * scale, 0.0))
        inverse.append(right[g] * scale)
    return jnp.concatenate(upper, axis=0), jnp.concatenate(inverse, axis=0)


def corner_kernel(corner_ref, low_ref, inv_ref, inv_t_ref):
    zero = jnp.zeros((TILE, TILE), jnp.float32)
    upper_0, inv_0 = factor_tile(corner_ref[:TILE, :TILE])
    low_10 = dot_full(corner_ref[TILE:, :TILE], inv_0, ((1,), (1,)))
    square = corner_ref[TILE:, TILE:] - dot_full(low_10, low_10, ((1,), (1,)))
    upper_1, inv_1 = factor_tile(square)
    inv_10 = -dot_full(inv_1, dot_full(low_10, inv_0))
    low_ref[:TILE, :TILE] = upper_0.T
    low_ref[:TILE, TILE:] = zero
    low_ref[TILE:, :TILE] = low_10
    low_ref[TILE:, TILE:] = upper_1.T
    first = jnp.concatenate([inv_0, zero], axis=1)
    second = jnp.concatenate([inv_10, inv_1], axis=1)
    inv_ref[...] = spread_halves(jnp.concatenate([first, second], axis=0))
    first = jnp.concatenate([inv_0.T, inv_10.T], axis=1)
    second = jnp.concatenate([zero, inv_1.T], axis=1)
    stack_halves(inv_t_ref, jnp.concatenate([first, second], axis=0))


def factor_corner(corner):
    return pl.pallas_call(
        corner_kernel,
        out_shape=(
            jax.ShapeDtypeStruct((WIDE, WIDE), jnp.float32),
            jax.ShapeDtypeStruct((WIDE, 3 * WIDE), jnp.bfloat16),
            jax.ShapeDtypeStruct((3 * WIDE, WIDE), jnp.bfloat16),
        ),
        compiler_params=pltpu.CompilerParams(vmem_limit_bytes=VMEM_LIMIT),
        cost_estimate=pl.CostEstimate(flops=40_000_000, bytes_accessed=1 << 20, transcendentals=0),
    )(corner)


def columns_kernel(info_ref, inv_ref, *refs):
    out_ref, stack = refs[-2:]
    odd = info_ref[0] % 2 == 1
    start = 0
    for mine_ref, other_ref in zip(refs[0:-2:2], refs[1:-2:2]):
        size = mine_ref.shape[1]
        here = pl.ds(start, size)
        mine, other = mine_ref[...], other_ref[...]
        first = jnp.where(odd, other, mine)
        second = jnp.where(odd, mine, other)
        stack_halves(stack.at[:, here], jnp.concatenate([first, second], axis=0))
        stack_halves(out_ref.at[:, here], dot_half(inv_ref[...], stack[:, here]))
        start += size


def solve_columns(info, inverse, pairs):
    flat = [array for pair in pairs for array in pair]
    total = sum(pair[0].shape[1] for pair in pairs)
    vmem = pl.BlockSpec(memory_space=pltpu.VMEM)
    return pl.pallas_call(
        columns_kernel,
        in_specs=[pl.BlockSpec(memory_space=pltpu.SMEM)] + [vmem] * (1 + len(flat)),
        out_specs=vmem,
        out_shape=jax.ShapeDtypeStruct((3 * WIDE, total), jnp.bfloat16),
        scratch_shapes=[pltpu.VMEM((3 * WIDE, total), jnp.bfloat16)],
        compiler_params=pltpu.CompilerParams(vmem_limit_bytes=VMEM_LIMIT),
        cost_estimate=pl.CostEstimate(
            flops=6 * WIDE * WIDE * total, bytes_accessed=WIDE * total * 8, transcendentals=0
        ),
    )(info, inverse, *flat)


def update_kernel(
    start, block, info_ref, mat_ref, right_ref, lower_ref, inv_t_ref, mine_ref, other_ref, *refs
):
    out_ref, taken, given, panel, first_panel, in_sems, out_sems = refs[-7:]
    row, core, col = info_ref[0], info_ref[2], info_ref[3]
    rows, columns = mine_ref.shape[0], mat_ref.shape[1]
    steps = columns // block
    part = next(p for p in (512, 256, TILE) if rows % p == 0)
    piece = rows // PIECES

    def across(step):
        return pl.ds(pl.multiple_of(step * block, TILE), block)

    def take(step, slot):
        for p in range(PIECES):
            pltpu.make_async_copy(
                mat_ref.at[pl.ds(start + p * piece, piece), across(step)],
                taken.at[slot, pl.ds(p * piece, piece)],
                in_sems.at[slot],
            ).start()

    def give(step, slot):
        for p in range(PIECES):
            pltpu.make_async_copy(
                given.at[slot, pl.ds(p * piece, piece)],
                out_ref.at[pl.ds(start + p * piece, piece), across(step)],
                out_sems.at[slot],
            ).start()

    def wait_taken(step, slot):
        whole = mat_ref.at[pl.ds(start, rows), across(step)]
        pltpu.make_async_copy(whole, taken.at[slot], in_sems.at[slot]).wait()

    def wait_given(step, slot):
        whole = out_ref.at[pl.ds(start, rows), across(step)]
        pltpu.make_async_copy(given.at[slot], whole, out_sems.at[slot]).wait()

    for step in range(min(IN_SLOTS, steps)):
        take(step, step)

    @pl.loop(0, rows // part)
    def _(index):
        here = pl.ds(pl.multiple_of(index * part, part), part)
        mine, other = mine_ref[here], other_ref[here]
        raw = jnp.concatenate(
            [jnp.where(core == 1, other, mine), jnp.where(core == 1, mine, other)], axis=1
        )
        solved = dot_half(spread_halves(raw), inv_t_ref[...])
        panel[here] = spread_halves(solved)
        first_panel[here] = jnp.where(col == 1, solved[:, TILE:], solved[:, :TILE])

    if start == 0:

        @pl.when(row < PANELS)
        def _():
            head = jnp.where(row == 0, lower_ref[:TILE], lower_ref[TILE:])
            panel[:TILE] = spread_halves(head)
            first_panel[:TILE] = jnp.where(col == 1, head[:, TILE:], head[:, :TILE])

    @pl.loop(0, steps)
    def _(step):
        in_slot, out_slot = lax.rem(step, IN_SLOTS), lax.rem(step, OUT_SLOTS)
        wait_taken(step, in_slot)

        @pl.when(step >= OUT_SLOTS)
        def _():
            wait_given(step - OUT_SLOTS, out_slot)

        @pl.loop(0, rows // part)
        def _(index):
            here = pl.ds(pl.multiple_of(index * part, part), part)
            product = dot_half(panel[here], right_ref[:, across(step)])
            given[out_slot, here] = taken[in_slot, here] - product

        if start == 0:

            @pl.when(row < PANELS)
            def _():
                given[out_slot, :TILE] = jnp.zeros((TILE, block), jnp.float32)

        @pl.when(jnp.logical_and(step == 0, col < PANELS))
        def _():
            given[out_slot, :, :TILE] = first_panel[...]

        give(step, out_slot)

        @pl.when(step + IN_SLOTS < steps)
        def _():
            take(step + IN_SLOTS, in_slot)

    for step in range(max(steps - OUT_SLOTS, 0), steps):
        wait_given(step, step % OUT_SLOTS)


def update_rows(start, info, matrix, right, lower, inv_t, mine, other, out):
    rows, columns = mine.shape[0], matrix.shape[1]
    block = next(b for b in (512, 640, 256, TILE) if columns % b == 0)
    any_spec = pl.BlockSpec(memory_space=pl.ANY)
    vmem = pl.BlockSpec(memory_space=pltpu.VMEM)
    in_specs = [pl.BlockSpec(memory_space=pltpu.SMEM), any_spec] + [vmem] * 5
    operands = [info, matrix, right, lower, inv_t, mine, other]
    aliases = {}
    if out is not None:
        aliases = {len(operands): 0}
        in_specs.append(any_spec)
        operands.append(out)
    return pl.pallas_call(
        functools.partial(update_kernel, start, block),
        in_specs=in_specs,
        out_specs=any_spec,
        out_shape=jax.ShapeDtypeStruct(matrix.shape, jnp.float32),
        scratch_shapes=[
            pltpu.VMEM((IN_SLOTS, rows, block), jnp.float32),
            pltpu.VMEM((OUT_SLOTS, rows, block), jnp.float32),
            pltpu.VMEM((rows, 3 * WIDE), jnp.bfloat16),
            pltpu.VMEM((rows, TILE), jnp.float32),
            pltpu.SemaphoreType.DMA((IN_SLOTS,)),
            pltpu.SemaphoreType.DMA((OUT_SLOTS,)),
        ],
        input_output_aliases=aliases,
        compiler_params=pltpu.CompilerParams(vmem_limit_bytes=VMEM_LIMIT),
        cost_estimate=pl.CostEstimate(
            flops=6 * rows * columns * WIDE,
            bytes_accessed=8 * rows * columns,
            transcendentals=0,
        ),
    )(*operands)


def after(value, *earlier):
    return lax.optimization_barrier((value, *earlier))[0]


def double_rows(block, row, row_count):
    stride = PANELS
    while stride < row_count:
        pairs = [(i, i + stride) for i in range(min(stride, row_count - stride))]
        got = lax.ppermute(block, "row", pairs)
        block = jnp.where(jnp.logical_and(row >= stride, row < 2 * stride), got, block)
        stride *= 2
    return block


def swap_rows(block, row_count):
    return lax.ppermute(block, "row", [(i, i ^ 1) for i in range(row_count)])


def pick(blocks, index):
    chosen = blocks[0]
    for shift in range(1, len(blocks)):
        chosen = jnp.where(index == shift, blocks[shift], chosen)
    return chosen


def share_corner(tile, earlier, row, place, core, row_count, col_count):
    depth = col_count // CORES
    got = [tile]
    for shift in range(1, row_count):
        pairs = [
            (p * col_count + c, (p + shift) % row_count * col_count + c)
            for p in range(PANELS)
            for c in range(CORES)
        ]
        got.append(lax.ppermute(tile, ("row", "col"), pairs))
    column = jnp.concatenate([pick(got, (row - p) % row_count) for p in range(PANELS)], axis=0)
    column = after(column, earlier)
    beside = lax.ppermute(column, "col", [(0, 1), (1, 0)])
    square = jnp.concatenate(
        [jnp.where(core == 0, column, beside), jnp.where(core == 0, beside, column)], axis=1
    )
    got = [square]
    for shift in range(1, depth):
        pairs = [(c, c + CORES * shift) for c in range(CORES)]
        got.append(lax.ppermute(square, "col", pairs))
    return column, square, pick(got, place)


def per_device(matrix):
    row_count = lax.axis_size("row")
    col_count = lax.axis_size("col")
    row = lax.axis_index("row")
    col = lax.axis_index("col")
    depth = col_count // CORES
    place, core = col // CORES, col % CORES
    info = jnp.stack([row, place, core, col]).astype(jnp.int32)
    tiles = matrix.shape[0] // TILE
    chunks = next(n for n in (5, 4, 2, 1) if tiles % n == 0)
    rows = tiles // chunks * TILE
    half = matrix.shape[1] // 2

    last = chunks + depth - 2
    held, got = [], None

    def fill(slot, *earlier):
        if slot < chunks:
            own = matrix[slot * rows : (slot + 1) * rows, :TILE]
            block = own if got is None else jnp.where(place == 0, own, got)
        else:
            block = got
        block = after(block, *earlier)
        held.append(block)
        if slot == last:
            return None
        busy = [c for c in range(col_count) if 0 <= slot - c // CORES < chunks]
        hops = [(c, c + CORES) for c in busy if c + CORES < col_count]
        return lax.ppermute(block, "col", hops)

    got = fill(0)
    tile = after(matrix[:TILE, :TILE], held[0])
    column, square, corner = share_corner(tile, got, row, place, core, row_count, col_count)
    bands = [after(matrix[:TILE, :half], column), after(matrix[:TILE, half:], column)]
    bands = [double_rows(band, row, row_count) for band in bands]
    got = fill(1, square)
    got = fill(2, bands[0], corner)
    lower, inverse, inv_t = factor_corner(after(corner, held[2]))
    besides = [swap_rows(band, row_count) for band in bands]
    slot = 3
    while slot < depth:
        got = fill(slot, inverse, bands[1], besides[0])
        slot += 1
    right = None
    out = None
    for chunk in range(chunks):
        mine = pick(held[chunk : chunk + depth], place)
        other = lax.ppermute(mine, "col", [(c, c ^ 1) for c in range(col_count)])
        if slot <= last:
            got = fill(slot) if out is None else fill(slot, out)
            slot += 1
        if right is None:
            right = solve_columns(info, inverse, list(zip(bands, besides)))
        other = after(other, held[-1])
        shared = (info, matrix, right, lower, inv_t)
        out = update_rows(chunk * rows, *shared, mine, other, out)
    return out


def solution(mesh):
    return jax.shard_map(
        per_device,
        mesh=mesh,
        in_specs=(P("row", "col"),),
        out_specs=P("row", "col"),
        check_vma=False,
    )
```

```python
import functools

import jax
import jax.numpy as jnp
from jax import lax
from jax.experimental import pallas as pl
from jax.experimental.pallas import tpu as pltpu
from jax.sharding import PartitionSpec as P

TILE = 128
PANELS = 2
WIDE = PANELS * TILE
CORES = 2
VMEM_LIMIT = 40 * 1024 * 1024
GROUP = 8
IN_SLOTS = 3
OUT_SLOTS = 2
PIECES = 4


def dot_full(left, right, dims=((1,), (0,))):
    return lax.dot_general(
        left,
        right,
        (dims, ((), ())),
        precision=lax.Precision.HIGHEST,
        preferred_element_type=jnp.float32,
    )


def dot_half(left, right):
    return lax.dot_general(
        left, right, (((1,), (0,)), ((), ())), preferred_element_type=jnp.float32
    )


def split_half(value):
    high = value.astype(jnp.bfloat16)
    low = (value - high.astype(jnp.float32)).astype(jnp.bfloat16)
    return high, low


def stack_halves(ref, value):
    high, low = split_half(value)
    ref[:WIDE] = high
    ref[WIDE : 2 * WIDE] = low
    ref[2 * WIDE :] = high


def spread_halves(value):
    high, low = split_half(value)
    return jnp.concatenate([high, high, low], axis=1)


def factor_tile(square):
    groups = TILE // GROUP
    shape = (GROUP, TILE)
    lane = lax.broadcasted_iota(jnp.int32, shape, 1)
    sub = lax.broadcasted_iota(jnp.int32, shape, 0)
    left = [square[g * GROUP : (g + 1) * GROUP] for g in range(groups)]
    right = [jnp.where(lane == sub + g * GROUP, 1.0, 0.0) for g in range(groups)]

    def row_of(value, index):
        return jnp.broadcast_to(value[index : index + 1], shape)

    def column_of(value, index):
        return jnp.broadcast_to(value[:, index : index + 1], shape)

    for g in range(groups):
        first = g * GROUP
        span = range(GROUP)
        columns = [column_of(left[g], first + b) for b in span]
        block = [[row_of(columns[b], a) if a <= b else None for b in span] for a in span]
        ratio = [[None] * GROUP for _ in span]
        inverse = []
        for s in span:
            inverse.append(1.0 / block[s][s])
            for t in range(s + 1, GROUP):
                ratio[t][s] = block[s][t] * inverse[s]
            for t in range(s + 1, GROUP):
                for b in range(t, GROUP):
                    block[t][b] = block[t][b] - ratio[t][s] * block[s][b]
        rows_left = [row_of(left[g], s) for s in span]
        rows_right = [row_of(right[g], s) for s in span]
        for t in span:
            for s in range(t):
                rows_left[t] = rows_left[t] - ratio[t][s] * rows_left[s]
                rows_right[t] = rows_right[t] - ratio[t][s] * rows_right[s]
        for s in span:
            left[g] = jnp.where(sub == s, rows_left[s], left[g])
            right[g] = jnp.where(sub == s, rows_right[s], right[g])
        rows_left = [rows_left[s] * inverse[s] for s in span]
        rows_right = [rows_right[s] * inverse[s] for s in span]
        for other in range(g + 1, groups):
            columns = [column_of(left[other], first + s) for s in span]
            for s in span:
                for t in range(s):
                    columns[s] = columns[s] - ratio[s][t] * columns[t]
            for s in span:
                left[other] = left[other] - columns[s] * rows_left[s]
                right[other] = right[other] - columns[s] * rows_right[s]
    upper, inverse = [], []
    for g in range(groups):
        row = sub + g * GROUP
        pivot = jnp.sum(jnp.where(lane == row, left[g], 0.0), axis=1, keepdims=True)
        scale = 1.0 / jnp.sqrt(pivot)
        upper.append(jnp.where(lane >= row, left[g] * scale, 0.0))
        inverse.append(right[g] * scale)
    return jnp.concatenate(upper, axis=0), jnp.concatenate(inverse, axis=0)


def corner_kernel(corner_ref, low_ref, inv_ref, inv_t_ref):
    zero = jnp.zeros((TILE, TILE), jnp.float32)
    upper_0, inv_0 = factor_tile(corner_ref[:TILE, :TILE])
    low_10 = dot_full(corner_ref[TILE:, :TILE], inv_0, ((1,), (1,)))
    square = corner_ref[TILE:, TILE:] - dot_full(low_10, low_10, ((1,), (1,)))
    upper_1, inv_1 = factor_tile(square)
    inv_10 = -dot_full(inv_1, dot_full(low_10, inv_0))
    low_ref[:TILE, :TILE] = upper_0.T
    low_ref[:TILE, TILE:] = zero
    low_ref[TILE:, :TILE] = low_10
    low_ref[TILE:, TILE:] = upper_1.T
    first = jnp.concatenate([inv_0, zero], axis=1)
    second = jnp.concatenate([inv_10, inv_1], axis=1)
    inv_ref[...] = spread_halves(jnp.concatenate([first, second], axis=0))
    first = jnp.concatenate([inv_0.T, inv_10.T], axis=1)
    second = jnp.concatenate([zero, inv_1.T], axis=1)
    stack_halves(inv_t_ref, jnp.concatenate([first, second], axis=0))


def factor_corner(corner):
    return pl.pallas_call(
        corner_kernel,
        out_shape=(
            jax.ShapeDtypeStruct((WIDE, WIDE), jnp.float32),
            jax.ShapeDtypeStruct((WIDE, 3 * WIDE), jnp.bfloat16),
            jax.ShapeDtypeStruct((3 * WIDE, WIDE), jnp.bfloat16),
        ),
        compiler_params=pltpu.CompilerParams(vmem_limit_bytes=VMEM_LIMIT),
        cost_estimate=pl.CostEstimate(flops=40_000_000, bytes_accessed=1 << 20, transcendentals=0),
    )(corner)


def columns_kernel(inv_ref, raw_ref, out_ref, stack):
    stack_halves(stack, raw_ref[...])
    stack_halves(out_ref, dot_half(inv_ref[...], stack[...]))


def solve_columns(inverse, bands):
    total = bands.shape[1]
    block = next(b for b in (512, 640, 256, TILE) if total % b == 0)
    return pl.pallas_call(
        columns_kernel,
        grid=(total // block,),
        in_specs=[
            pl.BlockSpec(memory_space=pltpu.VMEM),
            pl.BlockSpec((WIDE, block), lambda j: (0, j)),
        ],
        out_specs=pl.BlockSpec((3 * WIDE, block), lambda j: (0, j)),
        out_shape=jax.ShapeDtypeStruct((3 * WIDE, total), jnp.bfloat16),
        scratch_shapes=[pltpu.VMEM((3 * WIDE, block), jnp.bfloat16)],
        compiler_params=pltpu.CompilerParams(vmem_limit_bytes=VMEM_LIMIT),
        cost_estimate=pl.CostEstimate(
            flops=6 * WIDE * WIDE * total, bytes_accessed=WIDE * total * 8, transcendentals=0
        ),
    )(inverse, bands)


def update_kernel(
    start, block, info_ref, mat_ref, right_ref, lower_ref, inv_t_ref, mine_ref, other_ref, *refs
):
    out_ref, taken, given, panel, first_panel, in_sems, out_sems = refs[-7:]
    row, core, col = info_ref[0], info_ref[2], info_ref[3]
    rows, columns = mine_ref.shape[0], mat_ref.shape[1]
    steps = columns // block
    part = next(p for p in (512, 256, TILE) if rows % p == 0)
    piece = rows // PIECES

    def across(step):
        return pl.ds(pl.multiple_of(step * block, TILE), block)

    def take(step, slot):
        for p in range(PIECES):
            pltpu.make_async_copy(
                mat_ref.at[pl.ds(start + p * piece, piece), across(step)],
                taken.at[slot, pl.ds(p * piece, piece)],
                in_sems.at[slot],
            ).start()

    def give(step, slot):
        for p in range(PIECES):
            pltpu.make_async_copy(
                given.at[slot, pl.ds(p * piece, piece)],
                out_ref.at[pl.ds(start + p * piece, piece), across(step)],
                out_sems.at[slot],
            ).start()

    def wait_taken(step, slot):
        whole = mat_ref.at[pl.ds(start, rows), across(step)]
        pltpu.make_async_copy(whole, taken.at[slot], in_sems.at[slot]).wait()

    def wait_given(step, slot):
        whole = out_ref.at[pl.ds(start, rows), across(step)]
        pltpu.make_async_copy(given.at[slot], whole, out_sems.at[slot]).wait()

    for step in range(min(IN_SLOTS, steps)):
        take(step, step)

    @pl.loop(0, rows // part)
    def _(index):
        here = pl.ds(pl.multiple_of(index * part, part), part)
        mine, other = mine_ref[here], other_ref[here]
        raw = jnp.concatenate(
            [jnp.where(core == 1, other, mine), jnp.where(core == 1, mine, other)], axis=1
        )
        solved = dot_half(spread_halves(raw), inv_t_ref[...])
        panel[here] = spread_halves(solved)
        first_panel[here] = jnp.where(col == 1, solved[:, TILE:], solved[:, :TILE])

    if start == 0:

        @pl.when(row < PANELS)
        def _():
            head = jnp.where(row == 0, lower_ref[:TILE], lower_ref[TILE:])
            panel[:TILE] = spread_halves(head)
            first_panel[:TILE] = jnp.where(col == 1, head[:, TILE:], head[:, :TILE])

    @pl.loop(0, steps)
    def _(step):
        in_slot, out_slot = lax.rem(step, IN_SLOTS), lax.rem(step, OUT_SLOTS)
        wait_taken(step, in_slot)

        @pl.when(step >= OUT_SLOTS)
        def _():
            wait_given(step - OUT_SLOTS, out_slot)

        @pl.loop(0, rows // part)
        def _(index):
            here = pl.ds(pl.multiple_of(index * part, part), part)
            product = dot_half(panel[here], right_ref[:, across(step)])
            given[out_slot, here] = taken[in_slot, here] - product

        if start == 0:

            @pl.when(row < PANELS)
            def _():
                given[out_slot, :TILE] = jnp.zeros((TILE, block), jnp.float32)

        @pl.when(jnp.logical_and(step == 0, col < PANELS))
        def _():
            given[out_slot, :, :TILE] = first_panel[...]

        give(step, out_slot)

        @pl.when(step + IN_SLOTS < steps)
        def _():
            take(step + IN_SLOTS, in_slot)

    for step in range(max(steps - OUT_SLOTS, 0), steps):
        wait_given(step, step % OUT_SLOTS)


def update_rows(start, info, matrix, right, lower, inv_t, mine, other, out):
    rows, columns = mine.shape[0], matrix.shape[1]
    block = next(b for b in (512, 640, 256, TILE) if columns % b == 0)
    any_spec = pl.BlockSpec(memory_space=pl.ANY)
    vmem = pl.BlockSpec(memory_space=pltpu.VMEM)
    in_specs = [pl.BlockSpec(memory_space=pltpu.SMEM), any_spec] + [vmem] * 5
    operands = [info, matrix, right, lower, inv_t, mine, other]
    aliases = {}
    if out is not None:
        aliases = {len(operands): 0}
        in_specs.append(any_spec)
        operands.append(out)
    return pl.pallas_call(
        functools.partial(update_kernel, start, block),
        in_specs=in_specs,
        out_specs=any_spec,
        out_shape=jax.ShapeDtypeStruct(matrix.shape, jnp.float32),
        scratch_shapes=[
            pltpu.VMEM((IN_SLOTS, rows, block), jnp.float32),
            pltpu.VMEM((OUT_SLOTS, rows, block), jnp.float32),
            pltpu.VMEM((rows, 3 * WIDE), jnp.bfloat16),
            pltpu.VMEM((rows, TILE), jnp.float32),
            pltpu.SemaphoreType.DMA((IN_SLOTS,)),
            pltpu.SemaphoreType.DMA((OUT_SLOTS,)),
        ],
        input_output_aliases=aliases,
        compiler_params=pltpu.CompilerParams(vmem_limit_bytes=VMEM_LIMIT),
        cost_estimate=pl.CostEstimate(
            flops=6 * rows * columns * WIDE,
            bytes_accessed=8 * rows * columns,
            transcendentals=0,
        ),
    )(*operands)


def after(value, *earlier):
    return lax.optimization_barrier((value, *earlier))[0]


def pick(blocks, index):
    chosen = blocks[0]
    for shift in range(1, len(blocks)):
        chosen = jnp.where(index == shift, blocks[shift], chosen)
    return chosen


def share_tile(tile, row, row_count, col_count):
    got = [tile]
    for shift in range(1, row_count):
        pairs = [
            (p * col_count + c, (p + shift) % row_count * col_count + c)
            for p in range(PANELS)
            for c in range(CORES)
        ]
        got.append(lax.ppermute(tile, ("row", "col"), pairs))
    return jnp.concatenate([pick(got, (row - p) % row_count) for p in range(PANELS)], axis=0)


def share_corner(column, place, core, col_count):
    got = [column]
    for shift in range(1, col_count // CORES):
        pairs = [(c, c + CORES * shift) for c in range(CORES)]
        got.append(lax.ppermute(column, "col", pairs))
    column = pick(got, place)
    beside = lax.ppermute(column, "col", [(c, c ^ 1) for c in range(col_count)])
    halves = [jnp.where(core == 0, column, beside), jnp.where(core == 0, beside, column)]
    return column, jnp.concatenate(halves, axis=1)


def per_device(matrix):
    row_count = lax.axis_size("row")
    col_count = lax.axis_size("col")
    row = lax.axis_index("row")
    col = lax.axis_index("col")
    depth = col_count // CORES
    place, core = col // CORES, col % CORES
    info = jnp.stack([row, place, core, col]).astype(jnp.int32)
    tiles = matrix.shape[0] // TILE
    chunks = next(n for n in (5, 4, 2, 1) if tiles % n == 0)
    rows = tiles // chunks * TILE
    swap = [(c, c ^ 1) for c in range(col_count)]

    last = chunks + depth - 2
    held, got = [], None

    def fill(*earlier):
        slot = len(held)
        if slot < chunks:
            own = matrix[slot * rows : (slot + 1) * rows, :TILE]
            block = own if got is None else jnp.where(place == 0, own, got)
        else:
            block = got
        held.append(after(block, *earlier))
        busy = [c for c in range(col_count) if 0 <= slot - c // CORES < chunks]
        hops = [(c, c + CORES) for c in busy if c + CORES < col_count]
        return lax.ppermute(held[-1], "col", hops) if slot < last else None

    ready = []

    def exchange(*earlier):
        chunk = len(ready)
        mine = after(pick(held[chunk : chunk + depth], place), *earlier)
        ready.append((mine, lax.ppermute(mine, "col", swap)))
        return mine

    got = fill()
    tile = after(matrix[:TILE, :TILE], held[0])
    column = after(share_tile(tile, row, row_count, col_count), got)
    bands = lax.all_gather(after(matrix[:TILE], column), "row", axis=0, tiled=True)
    got = fill(column)
    column, corner = share_corner(after(column, held[1]), place, core, col_count)
    got = fill(column)
    while len(held) < depth:
        got = fill()
    mark = exchange()
    lower, inverse, inv_t = factor_corner(after(corner, held[-1], mark))
    got = fill(inverse)
    mark = exchange()
    right = solve_columns(inverse, bands)
    out = None
    for chunk in range(chunks):
        earlier = (mark,) if out is None else (mark, out)
        closing = len(held) == last
        if len(held) < last:
            got = fill(*earlier)
            mark = exchange(*earlier)
        mine, other = ready[chunk]
        other = after(other, held[-1], mark)
        out = update_rows(chunk * rows, info, matrix, right, lower, inv_t, mine, other, out)
        if closing:
            fill(out)
            mark = exchange(out)
    return out


def solution(mesh):
    return jax.shard_map(
        per_device,
        mesh=mesh,
        in_specs=(P("row", "col"),),
        out_specs=P("row", "col"),
        check_vma=False,
    )
```

```python
import functools

import jax
import jax.numpy as jnp
from jax import lax
from jax.experimental import pallas as pl
from jax.experimental.pallas import tpu as pltpu
from jax.sharding import PartitionSpec as P

TILE = 128
PANELS = 2
WIDE = PANELS * TILE
CORES = 2
VMEM_LIMIT = 40 * 1024 * 1024
GROUP = 8
IN_SLOTS = 5
OUT_SLOTS = 3
PIECES = 4


def dot_full(left, right, dims=((1,), (0,))):
    return lax.dot_general(
        left,
        right,
        (dims, ((), ())),
        precision=lax.Precision.HIGHEST,
        preferred_element_type=jnp.float32,
    )


def dot_half(left, right):
    return lax.dot_general(
        left, right, (((1,), (0,)), ((), ())), preferred_element_type=jnp.float32
    )


def split_half(value):
    high = value.astype(jnp.bfloat16)
    low = (value - high.astype(jnp.float32)).astype(jnp.bfloat16)
    return high, low


def stack_halves(ref, value):
    high, low = split_half(value)
    ref[:WIDE] = high
    ref[WIDE : 2 * WIDE] = low
    ref[2 * WIDE :] = high


def spread_halves(value):
    high, low = split_half(value)
    return jnp.concatenate([high, high, low], axis=1)


def factor_tile(square):
    groups = TILE // GROUP
    shape = (GROUP, TILE)
    lane = lax.broadcasted_iota(jnp.int32, shape, 1)
    sub = lax.broadcasted_iota(jnp.int32, shape, 0)
    left = [square[g * GROUP : (g + 1) * GROUP] for g in range(groups)]
    right = [jnp.where(lane == sub + g * GROUP, 1.0, 0.0) for g in range(groups)]

    def row_of(value, index):
        return jnp.broadcast_to(value[index : index + 1], shape)

    def column_of(value, index):
        return jnp.broadcast_to(value[:, index : index + 1], shape)

    for g in range(groups):
        first = g * GROUP
        span = range(GROUP)
        columns = [column_of(left[g], first + b) for b in span]
        block = [[row_of(columns[b], a) if a <= b else None for b in span] for a in span]
        ratio = [[None] * GROUP for _ in span]
        inverse = []
        for s in span:
            inverse.append(1.0 / block[s][s])
            for t in range(s + 1, GROUP):
                ratio[t][s] = block[s][t] * inverse[s]
            for t in range(s + 1, GROUP):
                for b in range(t, GROUP):
                    block[t][b] = block[t][b] - ratio[t][s] * block[s][b]
        rows_left = [row_of(left[g], s) for s in span]
        rows_right = [row_of(right[g], s) for s in span]
        for t in span:
            for s in range(t):
                rows_left[t] = rows_left[t] - ratio[t][s] * rows_left[s]
                rows_right[t] = rows_right[t] - ratio[t][s] * rows_right[s]
        for s in span:
            left[g] = jnp.where(sub == s, rows_left[s], left[g])
            right[g] = jnp.where(sub == s, rows_right[s], right[g])
        rows_left = [rows_left[s] * inverse[s] for s in span]
        rows_right = [rows_right[s] * inverse[s] for s in span]
        for other in range(g + 1, groups):
            columns = [column_of(left[other], first + s) for s in span]
            for s in span:
                for t in range(s):
                    columns[s] = columns[s] - ratio[s][t] * columns[t]
            for s in span:
                left[other] = left[other] - columns[s] * rows_left[s]
                right[other] = right[other] - columns[s] * rows_right[s]
    upper, inverse = [], []
    for g in range(groups):
        row = sub + g * GROUP
        pivot = jnp.sum(jnp.where(lane == row, left[g], 0.0), axis=1, keepdims=True)
        scale = 1.0 / jnp.sqrt(pivot)
        upper.append(jnp.where(lane >= row, left[g] * scale, 0.0))
        inverse.append(right[g] * scale)
    return jnp.concatenate(upper, axis=0), jnp.concatenate(inverse, axis=0)


def corner_kernel(corner_ref, low_ref, inv_ref, inv_t_ref):
    zero = jnp.zeros((TILE, TILE), jnp.float32)
    upper_0, inv_0 = factor_tile(corner_ref[:TILE, :TILE])
    low_10 = dot_full(corner_ref[TILE:, :TILE], inv_0, ((1,), (1,)))
    square = corner_ref[TILE:, TILE:] - dot_full(low_10, low_10, ((1,), (1,)))
    upper_1, inv_1 = factor_tile(square)
    inv_10 = -dot_full(inv_1, dot_full(low_10, inv_0))
    low_ref[:TILE, :TILE] = upper_0.T
    low_ref[:TILE, TILE:] = zero
    low_ref[TILE:, :TILE] = low_10
    low_ref[TILE:, TILE:] = upper_1.T
    first = jnp.concatenate([inv_0, zero], axis=1)
    second = jnp.concatenate([inv_10, inv_1], axis=1)
    inv_ref[...] = spread_halves(jnp.concatenate([first, second], axis=0))
    first = jnp.concatenate([inv_0.T, inv_10.T], axis=1)
    second = jnp.concatenate([zero, inv_1.T], axis=1)
    stack_halves(inv_t_ref, jnp.concatenate([first, second], axis=0))


def factor_corner(corner):
    return pl.pallas_call(
        corner_kernel,
        out_shape=(
            jax.ShapeDtypeStruct((WIDE, WIDE), jnp.float32),
            jax.ShapeDtypeStruct((WIDE, 3 * WIDE), jnp.bfloat16),
            jax.ShapeDtypeStruct((3 * WIDE, WIDE), jnp.bfloat16),
        ),
        compiler_params=pltpu.CompilerParams(vmem_limit_bytes=VMEM_LIMIT),
        cost_estimate=pl.CostEstimate(flops=40_000_000, bytes_accessed=1 << 20, transcendentals=0),
    )(corner)


def columns_kernel(info_ref, inv_ref, *refs):
    out_ref, stack = refs[-2:]
    odd = info_ref[0] % 2 == 1
    start = 0
    for mine_ref, other_ref in zip(refs[0:-2:2], refs[1:-2:2]):
        size = mine_ref.shape[1]
        here = pl.ds(start, size)
        mine, other = mine_ref[...], other_ref[...]
        first = jnp.where(odd, other, mine)
        second = jnp.where(odd, mine, other)
        stack_halves(stack.at[:, here], jnp.concatenate([first, second], axis=0))
        stack_halves(out_ref.at[:, here], dot_half(inv_ref[...], stack[:, here]))
        start += size


def solve_columns(info, inverse, pairs):
    flat = [array for pair in pairs for array in pair]
    total = sum(pair[0].shape[1] for pair in pairs)
    vmem = pl.BlockSpec(memory_space=pltpu.VMEM)
    return pl.pallas_call(
        columns_kernel,
        in_specs=[pl.BlockSpec(memory_space=pltpu.SMEM)] + [vmem] * (1 + len(flat)),
        out_specs=vmem,
        out_shape=jax.ShapeDtypeStruct((3 * WIDE, total), jnp.bfloat16),
        scratch_shapes=[pltpu.VMEM((3 * WIDE, total), jnp.bfloat16)],
        compiler_params=pltpu.CompilerParams(vmem_limit_bytes=VMEM_LIMIT),
        cost_estimate=pl.CostEstimate(
            flops=6 * WIDE * WIDE * total, bytes_accessed=WIDE * total * 8, transcendentals=0
        ),
    )(info, inverse, *flat)


def update_kernel(
    start, block, info_ref, mat_ref, right_ref, lower_ref, inv_t_ref, mine_ref, other_ref, *refs
):
    out_ref, taken, given, panel, first_panel, in_sems, out_sems = refs[-7:]
    row, core, col = info_ref[0], info_ref[2], info_ref[3]
    rows, columns = mine_ref.shape[0], mat_ref.shape[1]
    steps = columns // block
    part = next(p for p in (512, 256, TILE) if rows % p == 0)
    piece = rows // PIECES

    def across(step):
        return pl.ds(pl.multiple_of(step * block, TILE), block)

    def take(step, slot):
        for p in range(PIECES):
            pltpu.make_async_copy(
                mat_ref.at[pl.ds(start + p * piece, piece), across(step)],
                taken.at[slot, pl.ds(p * piece, piece)],
                in_sems.at[slot],
            ).start()

    def give(step, slot):
        for p in range(PIECES):
            pltpu.make_async_copy(
                given.at[slot, pl.ds(p * piece, piece)],
                out_ref.at[pl.ds(start + p * piece, piece), across(step)],
                out_sems.at[slot],
            ).start()

    def wait_taken(step, slot):
        whole = mat_ref.at[pl.ds(start, rows), across(step)]
        pltpu.make_async_copy(whole, taken.at[slot], in_sems.at[slot]).wait()

    def wait_given(step, slot):
        whole = out_ref.at[pl.ds(start, rows), across(step)]
        pltpu.make_async_copy(given.at[slot], whole, out_sems.at[slot]).wait()

    for step in range(min(IN_SLOTS, steps)):
        take(step, step)

    @pl.loop(0, rows // part)
    def _(index):
        here = pl.ds(pl.multiple_of(index * part, part), part)
        mine, other = mine_ref[here], other_ref[here]
        raw = jnp.concatenate(
            [jnp.where(core == 1, other, mine), jnp.where(core == 1, mine, other)], axis=1
        )
        solved = dot_half(spread_halves(raw), inv_t_ref[...])
        panel[here] = spread_halves(solved)
        first_panel[here] = jnp.where(col == 1, solved[:, TILE:], solved[:, :TILE])

    if start == 0:

        @pl.when(row < PANELS)
        def _():
            head = jnp.where(row == 0, lower_ref[:TILE], lower_ref[TILE:])
            panel[:TILE] = spread_halves(head)
            first_panel[:TILE] = jnp.where(col == 1, head[:, TILE:], head[:, :TILE])

    @pl.loop(0, steps)
    def _(step):
        in_slot, out_slot = lax.rem(step, IN_SLOTS), lax.rem(step, OUT_SLOTS)
        wait_taken(step, in_slot)

        @pl.when(step >= OUT_SLOTS)
        def _():
            wait_given(step - OUT_SLOTS, out_slot)

        @pl.loop(0, rows // part)
        def _(index):
            here = pl.ds(pl.multiple_of(index * part, part), part)
            product = dot_half(panel[here], right_ref[:, across(step)])
            given[out_slot, here] = taken[in_slot, here] - product

        if start == 0:

            @pl.when(row < PANELS)
            def _():
                given[out_slot, :TILE] = jnp.zeros((TILE, block), jnp.float32)

        @pl.when(jnp.logical_and(step == 0, col < PANELS))
        def _():
            given[out_slot, :, :TILE] = first_panel[...]

        give(step, out_slot)

        @pl.when(step + IN_SLOTS < steps)
        def _():
            take(step + IN_SLOTS, in_slot)

    for step in range(max(steps - OUT_SLOTS, 0), steps):
        wait_given(step, step % OUT_SLOTS)


def update_rows(start, info, matrix, right, lower, inv_t, mine, other, out):
    rows, columns = mine.shape[0], matrix.shape[1]
    block = 2 * TILE if columns % (2 * TILE) == 0 else TILE
    any_spec = pl.BlockSpec(memory_space=pl.ANY)
    vmem = pl.BlockSpec(memory_space=pltpu.VMEM)
    in_specs = [pl.BlockSpec(memory_space=pltpu.SMEM), any_spec] + [vmem] * 5
    operands = [info, matrix, right, lower, inv_t, mine, other]
    aliases = {}
    if out is not None:
        aliases = {len(operands): 0}
        in_specs.append(any_spec)
        operands.append(out)
    return pl.pallas_call(
        functools.partial(update_kernel, start, block),
        in_specs=in_specs,
        out_specs=any_spec,
        out_shape=jax.ShapeDtypeStruct(matrix.shape, jnp.float32),
        scratch_shapes=[
            pltpu.VMEM((IN_SLOTS, rows, block), jnp.float32),
            pltpu.VMEM((OUT_SLOTS, rows, block), jnp.float32),
            pltpu.VMEM((rows, 3 * WIDE), jnp.bfloat16),
            pltpu.VMEM((rows, TILE), jnp.float32),
            pltpu.SemaphoreType.DMA((IN_SLOTS,)),
            pltpu.SemaphoreType.DMA((OUT_SLOTS,)),
        ],
        input_output_aliases=aliases,
        compiler_params=pltpu.CompilerParams(vmem_limit_bytes=VMEM_LIMIT),
        cost_estimate=pl.CostEstimate(
            flops=6 * rows * columns * WIDE,
            bytes_accessed=8 * rows * columns,
            transcendentals=0,
        ),
    )(*operands)


def after(value, *earlier):
    return lax.optimization_barrier((value, *earlier))[0]


def double_rows(block, row, row_count):
    stride = PANELS
    while stride < row_count:
        pairs = [(i, i + stride) for i in range(min(stride, row_count - stride))]
        got = lax.ppermute(block, "row", pairs)
        block = jnp.where(jnp.logical_and(row >= stride, row < 2 * stride), got, block)
        stride *= 2
    return block


def swap_rows(block, row_count):
    return lax.ppermute(block, "row", [(i, i ^ 1) for i in range(row_count)])


def pick(blocks, index):
    chosen = blocks[0]
    for shift in range(1, len(blocks)):
        chosen = jnp.where(index == shift, blocks[shift], chosen)
    return chosen


def share_tile(tile, row, row_count, col_count):
    got = [tile]
    for shift in range(1, row_count):
        pairs = [
            (p * col_count + c, (p + shift) % row_count * col_count + c)
            for p in range(PANELS)
            for c in range(CORES)
        ]
        got.append(lax.ppermute(tile, ("row", "col"), pairs))
    return jnp.concatenate([pick(got, (row - p) % row_count) for p in range(PANELS)], axis=0)


def share_corner(column, place, core, col_count):
    got = [column]
    for shift in range(1, col_count // CORES):
        pairs = [(c, c + CORES * shift) for c in range(CORES)]
        got.append(lax.ppermute(column, "col", pairs))
    column = pick(got, place)
    beside = lax.ppermute(column, "col", [(c, c ^ 1) for c in range(col_count)])
    halves = [jnp.where(core == 0, column, beside), jnp.where(core == 0, beside, column)]
    return column, jnp.concatenate(halves, axis=1)


def per_device(matrix):
    row_count = lax.axis_size("row")
    col_count = lax.axis_size("col")
    row = lax.axis_index("row")
    col = lax.axis_index("col")
    depth = col_count // CORES
    place, core = col // CORES, col % CORES
    info = jnp.stack([row, place, core, col]).astype(jnp.int32)
    tiles = matrix.shape[0] // TILE
    chunks = next(n for n in (5, 4, 2, 1) if tiles % n == 0)
    rows = tiles // chunks * TILE
    half = matrix.shape[1] // 2
    swap = [(c, c ^ 1) for c in range(col_count)]

    last = chunks + depth - 2
    held, got = [], None

    def fill(*earlier):
        slot = len(held)
        if slot < chunks:
            own = matrix[slot * rows : (slot + 1) * rows, :TILE]
            block = own if got is None else jnp.where(place == 0, own, got)
        else:
            block = got
        held.append(after(block, *earlier))
        busy = [c for c in range(col_count) if 0 <= slot - c // CORES < chunks]
        hops = [(c, c + CORES) for c in busy if c + CORES < col_count]
        return lax.ppermute(held[-1], "col", hops) if slot < last else None

    ready = []

    def exchange(*earlier):
        chunk = len(ready)
        mine = after(pick(held[chunk : chunk + depth], place), *earlier)
        ready.append((mine, lax.ppermute(mine, "col", swap)))
        return mine

    got = fill()
    tile = after(matrix[:TILE, :TILE], held[0])
    column = after(share_tile(tile, row, row_count, col_count), got)
    got = fill(column)
    bands = [after(matrix[:TILE, :half], held[1]), after(matrix[:TILE, half:], held[1])]
    column = after(column, *bands)
    bands = [double_rows(band, row, row_count) for band in bands]
    column, corner = share_corner(column, place, core, col_count)
    got = fill(column, bands[0])
    while len(held) < depth:
        got = fill()
    mark = exchange()
    besides = [swap_rows(band, row_count) for band in bands]
    lower, inverse, inv_t = factor_corner(after(corner, held[-1], mark, bands[1]))
    got = fill(inverse, ready[0][1], besides[0])
    mark = exchange()
    right = solve_columns(info, inverse, list(zip(bands, besides)))
    out = None
    for chunk in range(chunks):
        earlier = (mark,) if out is None else (mark, out)
        closing = len(held) == last
        if len(held) < last:
            got = fill(*earlier)
            mark = exchange(*earlier)
        mine, other = ready[chunk]
        other = after(other, held[-1], mark)
        out = update_rows(chunk * rows, info, matrix, right, lower, inv_t, mine, other, out)
        if closing:
            fill(out)
            mark = exchange(out)
    return out


def solution(mesh):
    return jax.shard_map(
        per_device,
        mesh=mesh,
        in_specs=(P("row", "col"),),
        out_specs=P("row", "col"),
        check_vma=False,
    )
```

```python
import functools

import jax
import jax.numpy as jnp
from jax import lax
from jax.experimental import pallas as pl
from jax.experimental.pallas import tpu as pltpu
from jax.sharding import PartitionSpec as P

TILE = 128
PANELS = 2
WIDE = PANELS * TILE
CORES = 2
VMEM_LIMIT = 40 * 1024 * 1024
GROUP = 8
IN_SLOTS = 3
OUT_SLOTS = 2
PIECES = 4


def dot_full(left, right, dims=((1,), (0,))):
    return lax.dot_general(
        left,
        right,
        (dims, ((), ())),
        precision=lax.Precision.HIGHEST,
        preferred_element_type=jnp.float32,
    )


def dot_half(left, right):
    return lax.dot_general(
        left, right, (((1,), (0,)), ((), ())), preferred_element_type=jnp.float32
    )


def split_half(value):
    high = value.astype(jnp.bfloat16)
    low = (value - high.astype(jnp.float32)).astype(jnp.bfloat16)
    return high, low


def stack_halves(ref, value):
    high, low = split_half(value)
    ref[:WIDE] = high
    ref[WIDE : 2 * WIDE] = low
    ref[2 * WIDE :] = high


def spread_halves(value):
    high, low = split_half(value)
    return jnp.concatenate([high, high, low], axis=1)


def factor_tile(square):
    groups = TILE // GROUP
    shape = (GROUP, TILE)
    lane = lax.broadcasted_iota(jnp.int32, shape, 1)
    sub = lax.broadcasted_iota(jnp.int32, shape, 0)
    left = [square[g * GROUP : (g + 1) * GROUP] for g in range(groups)]
    right = [jnp.where(lane == sub + g * GROUP, 1.0, 0.0) for g in range(groups)]

    def row_of(value, index):
        return jnp.broadcast_to(value[index : index + 1], shape)

    def column_of(value, index):
        return jnp.broadcast_to(value[:, index : index + 1], shape)

    for g in range(groups):
        first = g * GROUP
        span = range(GROUP)
        columns = [column_of(left[g], first + b) for b in span]
        block = [[row_of(columns[b], a) if a <= b else None for b in span] for a in span]
        ratio = [[None] * GROUP for _ in span]
        inverse = []
        for s in span:
            inverse.append(1.0 / block[s][s])
            for t in range(s + 1, GROUP):
                ratio[t][s] = block[s][t] * inverse[s]
            for t in range(s + 1, GROUP):
                for b in range(t, GROUP):
                    block[t][b] = block[t][b] - ratio[t][s] * block[s][b]
        rows_left = [row_of(left[g], s) for s in span]
        rows_right = [row_of(right[g], s) for s in span]
        for t in span:
            for s in range(t):
                rows_left[t] = rows_left[t] - ratio[t][s] * rows_left[s]
                rows_right[t] = rows_right[t] - ratio[t][s] * rows_right[s]
        for s in span:
            left[g] = jnp.where(sub == s, rows_left[s], left[g])
            right[g] = jnp.where(sub == s, rows_right[s], right[g])
        rows_left = [rows_left[s] * inverse[s] for s in span]
        rows_right = [rows_right[s] * inverse[s] for s in span]
        for other in range(g + 1, groups):
            columns = [column_of(left[other], first + s) for s in span]
            for s in span:
                for t in range(s):
                    columns[s] = columns[s] - ratio[s][t] * columns[t]
            for s in span:
                left[other] = left[other] - columns[s] * rows_left[s]
                right[other] = right[other] - columns[s] * rows_right[s]
    upper, inverse = [], []
    for g in range(groups):
        row = sub + g * GROUP
        pivot = jnp.sum(jnp.where(lane == row, left[g], 0.0), axis=1, keepdims=True)
        scale = 1.0 / jnp.sqrt(pivot)
        upper.append(jnp.where(lane >= row, left[g] * scale, 0.0))
        inverse.append(right[g] * scale)
    return jnp.concatenate(upper, axis=0), jnp.concatenate(inverse, axis=0)


def corner_kernel(corner_ref, low_ref, inv_ref, inv_t_ref):
    zero = jnp.zeros((TILE, TILE), jnp.float32)
    upper_0, inv_0 = factor_tile(corner_ref[:TILE, :TILE])
    low_10 = dot_full(corner_ref[TILE:, :TILE], inv_0, ((1,), (1,)))
    square = corner_ref[TILE:, TILE:] - dot_full(low_10, low_10, ((1,), (1,)))
    upper_1, inv_1 = factor_tile(square)
    inv_10 = -dot_full(inv_1, dot_full(low_10, inv_0))
    low_ref[:TILE, :TILE] = upper_0.T
    low_ref[:TILE, TILE:] = zero
    low_ref[TILE:, :TILE] = low_10
    low_ref[TILE:, TILE:] = upper_1.T
    first = jnp.concatenate([inv_0, zero], axis=1)
    second = jnp.concatenate([inv_10, inv_1], axis=1)
    inv_ref[...] = spread_halves(jnp.concatenate([first, second], axis=0))
    first = jnp.concatenate([inv_0.T, inv_10.T], axis=1)
    second = jnp.concatenate([zero, inv_1.T], axis=1)
    stack_halves(inv_t_ref, jnp.concatenate([first, second], axis=0))


def factor_corner(corner):
    return pl.pallas_call(
        corner_kernel,
        out_shape=(
            jax.ShapeDtypeStruct((WIDE, WIDE), jnp.float32),
            jax.ShapeDtypeStruct((WIDE, 3 * WIDE), jnp.bfloat16),
            jax.ShapeDtypeStruct((3 * WIDE, WIDE), jnp.bfloat16),
        ),
        compiler_params=pltpu.CompilerParams(vmem_limit_bytes=VMEM_LIMIT),
        cost_estimate=pl.CostEstimate(flops=40_000_000, bytes_accessed=1 << 20, transcendentals=0),
    )(corner)


def columns_kernel(info_ref, inv_ref, *refs):
    out_ref, stack = refs[-2:]
    odd = info_ref[0] % 2 == 1
    start = 0
    for mine_ref, other_ref in zip(refs[0:-2:2], refs[1:-2:2]):
        size = mine_ref.shape[1]
        here = pl.ds(start, size)
        mine, other = mine_ref[...], other_ref[...]
        first = jnp.where(odd, other, mine)
        second = jnp.where(odd, mine, other)
        stack_halves(stack.at[:, here], jnp.concatenate([first, second], axis=0))
        stack_halves(out_ref.at[:, here], dot_half(inv_ref[...], stack[:, here]))
        start += size


def solve_columns(info, inverse, pairs):
    flat = [array for pair in pairs for array in pair]
    total = sum(pair[0].shape[1] for pair in pairs)
    vmem = pl.BlockSpec(memory_space=pltpu.VMEM)
    return pl.pallas_call(
        columns_kernel,
        in_specs=[pl.BlockSpec(memory_space=pltpu.SMEM)] + [vmem] * (1 + len(flat)),
        out_specs=vmem,
        out_shape=jax.ShapeDtypeStruct((3 * WIDE, total), jnp.bfloat16),
        scratch_shapes=[pltpu.VMEM((3 * WIDE, total), jnp.bfloat16)],
        compiler_params=pltpu.CompilerParams(vmem_limit_bytes=VMEM_LIMIT),
        cost_estimate=pl.CostEstimate(
            flops=6 * WIDE * WIDE * total, bytes_accessed=WIDE * total * 8, transcendentals=0
        ),
    )(info, inverse, *flat)


def update_kernel(
    start, block, info_ref, mat_ref, right_ref, lower_ref, inv_t_ref, mine_ref, other_ref, *refs
):
    out_ref, taken, given, panel, first_panel, in_sems, out_sems = refs[-7:]
    row, core, col = info_ref[0], info_ref[2], info_ref[3]
    rows, columns = mine_ref.shape[0], mat_ref.shape[1]
    steps = columns // block
    part = next(p for p in (512, 256, TILE) if rows % p == 0)
    piece = rows // PIECES

    def across(step):
        return pl.ds(pl.multiple_of(step * block, TILE), block)

    def take(step, slot):
        for p in range(PIECES):
            pltpu.make_async_copy(
                mat_ref.at[pl.ds(start + p * piece, piece), across(step)],
                taken.at[slot, pl.ds(p * piece, piece)],
                in_sems.at[slot],
            ).start()

    def give(step, slot):
        for p in range(PIECES):
            pltpu.make_async_copy(
                given.at[slot, pl.ds(p * piece, piece)],
                out_ref.at[pl.ds(start + p * piece, piece), across(step)],
                out_sems.at[slot],
            ).start()

    def wait_taken(step, slot):
        whole = mat_ref.at[pl.ds(start, rows), across(step)]
        pltpu.make_async_copy(whole, taken.at[slot], in_sems.at[slot]).wait()

    def wait_given(step, slot):
        whole = out_ref.at[pl.ds(start, rows), across(step)]
        pltpu.make_async_copy(given.at[slot], whole, out_sems.at[slot]).wait()

    for step in range(min(IN_SLOTS, steps)):
        take(step, step)

    @pl.loop(0, rows // part)
    def _(index):
        here = pl.ds(pl.multiple_of(index * part, part), part)
        mine, other = mine_ref[here], other_ref[here]
        raw = jnp.concatenate(
            [jnp.where(core == 1, other, mine), jnp.where(core == 1, mine, other)], axis=1
        )
        solved = dot_half(spread_halves(raw), inv_t_ref[...])
        panel[here] = spread_halves(solved)
        first_panel[here] = jnp.where(col == 1, solved[:, TILE:], solved[:, :TILE])

    if start == 0:

        @pl.when(row < PANELS)
        def _():
            head = jnp.where(row == 0, lower_ref[:TILE], lower_ref[TILE:])
            panel[:TILE] = spread_halves(head)
            first_panel[:TILE] = jnp.where(col == 1, head[:, TILE:], head[:, :TILE])

    @pl.loop(0, steps)
    def _(step):
        in_slot, out_slot = lax.rem(step, IN_SLOTS), lax.rem(step, OUT_SLOTS)
        wait_taken(step, in_slot)

        @pl.when(step >= OUT_SLOTS)
        def _():
            wait_given(step - OUT_SLOTS, out_slot)

        @pl.loop(0, rows // part)
        def _(index):
            here = pl.ds(pl.multiple_of(index * part, part), part)
            product = dot_half(panel[here], right_ref[:, across(step)])
            given[out_slot, here] = taken[in_slot, here] - product

        if start == 0:

            @pl.when(row < PANELS)
            def _():
                given[out_slot, :TILE] = jnp.zeros((TILE, block), jnp.float32)

        @pl.when(jnp.logical_and(step == 0, col < PANELS))
        def _():
            given[out_slot, :, :TILE] = first_panel[...]

        give(step, out_slot)

        @pl.when(step + IN_SLOTS < steps)
        def _():
            take(step + IN_SLOTS, in_slot)

    for step in range(max(steps - OUT_SLOTS, 0), steps):
        wait_given(step, step % OUT_SLOTS)


def update_rows(start, info, matrix, right, lower, inv_t, mine, other, out):
    rows, columns = mine.shape[0], matrix.shape[1]
    block = next(b for b in (512, 640, 256, TILE) if columns % b == 0)
    any_spec = pl.BlockSpec(memory_space=pl.ANY)
    vmem = pl.BlockSpec(memory_space=pltpu.VMEM)
    in_specs = [pl.BlockSpec(memory_space=pltpu.SMEM), any_spec] + [vmem] * 5
    operands = [info, matrix, right, lower, inv_t, mine, other]
    aliases = {}
    if out is not None:
        aliases = {len(operands): 0}
        in_specs.append(any_spec)
        operands.append(out)
    return pl.pallas_call(
        functools.partial(update_kernel, start, block),
        in_specs=in_specs,
        out_specs=any_spec,
        out_shape=jax.ShapeDtypeStruct(matrix.shape, jnp.float32),
        scratch_shapes=[
            pltpu.VMEM((IN_SLOTS, rows, block), jnp.float32),
            pltpu.VMEM((OUT_SLOTS, rows, block), jnp.float32),
            pltpu.VMEM((rows, 3 * WIDE), jnp.bfloat16),
            pltpu.VMEM((rows, TILE), jnp.float32),
            pltpu.SemaphoreType.DMA((IN_SLOTS,)),
            pltpu.SemaphoreType.DMA((OUT_SLOTS,)),
        ],
        input_output_aliases=aliases,
        compiler_params=pltpu.CompilerParams(vmem_limit_bytes=VMEM_LIMIT),
        cost_estimate=pl.CostEstimate(
            flops=6 * rows * columns * WIDE,
            bytes_accessed=8 * rows * columns,
            transcendentals=0,
        ),
    )(*operands)


def after(value, *earlier):
    return lax.optimization_barrier((value, *earlier))[0]


def double_rows(block, row, row_count, *earlier):
    stride = PANELS
    while stride < row_count:
        pairs = [(i, i + stride) for i in range(min(stride, row_count - stride))]
        got = after(lax.ppermute(block, "row", pairs), *earlier)
        block = jnp.where(jnp.logical_and(row >= stride, row < 2 * stride), got, block)
        stride *= 2
    return block


def swap_rows(block, row_count):
    return lax.ppermute(block, "row", [(i, i ^ 1) for i in range(row_count)])


def pick(blocks, index):
    chosen = blocks[0]
    for shift in range(1, len(blocks)):
        chosen = jnp.where(index == shift, blocks[shift], chosen)
    return chosen


def share_tile(tile, row, row_count, col_count):
    got = [tile]
    for shift in range(1, row_count):
        pairs = [
            (p * col_count + c, (p + shift) % row_count * col_count + c)
            for p in range(PANELS)
            for c in range(CORES)
        ]
        got.append(lax.ppermute(tile, ("row", "col"), pairs))
    return jnp.concatenate([pick(got, (row - p) % row_count) for p in range(PANELS)], axis=0)


def share_corner(column, earlier, place, core, col_count):
    got = [column]
    for shift in range(1, col_count // CORES):
        pairs = [(c, c + CORES * shift) for c in range(CORES)]
        got.append(lax.ppermute(column, "col", pairs))
    column = after(pick(got, place), earlier)
    beside = lax.ppermute(column, "col", [(c, c ^ 1) for c in range(col_count)])
    halves = [jnp.where(core == 0, column, beside), jnp.where(core == 0, beside, column)]
    return jnp.concatenate(halves, axis=1)


def per_device(matrix):
    row_count = lax.axis_size("row")
    col_count = lax.axis_size("col")
    row = lax.axis_index("row")
    col = lax.axis_index("col")
    depth = col_count // CORES
    place, core = col // CORES, col % CORES
    info = jnp.stack([row, place, core, col]).astype(jnp.int32)
    tiles = matrix.shape[0] // TILE
    chunks = next(n for n in (5, 4, 2, 1) if tiles % n == 0)
    rows = tiles // chunks * TILE
    half = matrix.shape[1] // 2
    swap = [(c, c ^ 1) for c in range(col_count)]

    last = chunks + depth - 2
    held, got = [], None

    def fill(*earlier):
        slot = len(held)
        if slot < chunks:
            own = matrix[slot * rows : (slot + 1) * rows, :TILE]
            block = own if got is None else jnp.where(place == 0, own, got)
        else:
            block = got
        held.append(after(block, *earlier))
        busy = [c for c in range(col_count) if 0 <= slot - c // CORES < chunks]
        hops = [(c, c + CORES) for c in busy if c + CORES < col_count]
        return lax.ppermute(held[-1], "col", hops) if slot < last else None

    ready = []

    def exchange(*earlier):
        chunk = len(ready)
        mine = after(pick(held[chunk : chunk + depth], place), *earlier)
        ready.append((mine, lax.ppermute(mine, "col", swap)))
        return mine

    got = fill()
    tile = after(matrix[:TILE, :TILE], held[0])
    column = after(share_tile(tile, row, row_count, col_count), got)
    got = fill(column)
    bands = [after(matrix[:TILE, :half], held[1]), after(matrix[:TILE, half:], held[1])]
    column = after(column, *bands)
    bands[0] = double_rows(bands[0], row, row_count)
    corner = share_corner(column, bands[0], place, core, col_count)
    got = fill()
    while len(held) < depth:
        got = fill(corner)
    bands[1] = double_rows(bands[1], row, row_count, corner)
    besides = [swap_rows(band, row_count) for band in bands]
    mark = exchange()
    lower, inverse, inv_t = factor_corner(after(corner, held[-1], mark, bands[1]))
    got = fill(inverse, besides[0])
    mark = exchange()
    right = solve_columns(info, after(inverse, held[-1]), list(zip(bands, besides)))
    out = None
    for chunk in range(chunks):
        mine, other = ready[chunk]
        other = after(other, held[-1], mark)
        out = update_rows(chunk * rows, info, matrix, right, lower, inv_t, mine, other, out)
        if len(held) <= last:
            got = fill(mark, out)
            mark = exchange(out)
    return out


def solution(mesh):
    return jax.shard_map(
        per_device,
        mesh=mesh,
        in_specs=(P("row", "col"),),
        out_specs=P("row", "col"),
        check_vma=False,
    )
```

```python
import functools

import jax
import jax.numpy as jnp
from jax import lax
from jax.experimental import pallas as pl
from jax.experimental.pallas import tpu as pltpu
from jax.sharding import PartitionSpec as P

TILE = 128
PANELS = 2
WIDE = PANELS * TILE
CORES = 2
VMEM_LIMIT = 40 * 1024 * 1024
GROUP = 8
IN_SLOTS = 3
OUT_SLOTS = 2
PIECES = 4


def dot_full(left, right, dims=((1,), (0,))):
    return lax.dot_general(
        left,
        right,
        (dims, ((), ())),
        precision=lax.Precision.HIGHEST,
        preferred_element_type=jnp.float32,
    )


def dot_half(left, right):
    return lax.dot_general(
        left, right, (((1,), (0,)), ((), ())), preferred_element_type=jnp.float32
    )


def split_half(value):
    high = value.astype(jnp.bfloat16)
    low = (value - high.astype(jnp.float32)).astype(jnp.bfloat16)
    return high, low


def stack_halves(ref, value):
    high, low = split_half(value)
    ref[:WIDE] = high
    ref[WIDE : 2 * WIDE] = low
    ref[2 * WIDE :] = high


def spread_halves(value):
    high, low = split_half(value)
    return jnp.concatenate([high, high, low], axis=1)


def factor_tile(square):
    groups = TILE // GROUP
    shape = (GROUP, TILE)
    lane = lax.broadcasted_iota(jnp.int32, shape, 1)
    sub = lax.broadcasted_iota(jnp.int32, shape, 0)
    left = [square[g * GROUP : (g + 1) * GROUP] for g in range(groups)]
    right = [jnp.where(lane == sub + g * GROUP, 1.0, 0.0) for g in range(groups)]

    def row_of(value, index):
        return jnp.broadcast_to(value[index : index + 1], shape)

    def column_of(value, index):
        return jnp.broadcast_to(value[:, index : index + 1], shape)

    for g in range(groups):
        first = g * GROUP
        span = range(GROUP)
        columns = [column_of(left[g], first + b) for b in span]
        block = [[row_of(columns[b], a) if a <= b else None for b in span] for a in span]
        ratio = [[None] * GROUP for _ in span]
        inverse = []
        for s in span:
            inverse.append(1.0 / block[s][s])
            for t in range(s + 1, GROUP):
                ratio[t][s] = block[s][t] * inverse[s]
            for t in range(s + 1, GROUP):
                for b in range(t, GROUP):
                    block[t][b] = block[t][b] - ratio[t][s] * block[s][b]
        rows_left = [row_of(left[g], s) for s in span]
        rows_right = [row_of(right[g], s) for s in span]
        for t in span:
            for s in range(t):
                rows_left[t] = rows_left[t] - ratio[t][s] * rows_left[s]
                rows_right[t] = rows_right[t] - ratio[t][s] * rows_right[s]
        for s in span:
            left[g] = jnp.where(sub == s, rows_left[s], left[g])
            right[g] = jnp.where(sub == s, rows_right[s], right[g])
        rows_left = [rows_left[s] * inverse[s] for s in span]
        rows_right = [rows_right[s] * inverse[s] for s in span]
        for other in range(g + 1, groups):
            columns = [column_of(left[other], first + s) for s in span]
            for s in span:
                for t in range(s):
                    columns[s] = columns[s] - ratio[s][t] * columns[t]
            for s in span:
                left[other] = left[other] - columns[s] * rows_left[s]
                right[other] = right[other] - columns[s] * rows_right[s]
    upper, inverse = [], []
    for g in range(groups):
        row = sub + g * GROUP
        pivot = jnp.sum(jnp.where(lane == row, left[g], 0.0), axis=1, keepdims=True)
        scale = 1.0 / jnp.sqrt(pivot)
        upper.append(jnp.where(lane >= row, left[g] * scale, 0.0))
        inverse.append(right[g] * scale)
    return jnp.concatenate(upper, axis=0), jnp.concatenate(inverse, axis=0)


def first_kernel(corner_ref, upper_ref, inv_ref, low_ref, square_ref):
    upper, inverse = factor_tile(corner_ref[:TILE, :TILE])
    low = dot_full(corner_ref[TILE:, :TILE], inverse, ((1,), (1,)))
    upper_ref[...] = upper
    inv_ref[...] = inverse
    low_ref[...] = low
    square_ref[...] = corner_ref[TILE:, TILE:] - dot_full(low, low, ((1,), (1,)))


def second_kernel(upper_ref, inv_0_ref, low_10_ref, square_ref, low_ref, inv_ref, inv_t_ref):
    zero = jnp.zeros((TILE, TILE), jnp.float32)
    inv_0, low_10 = inv_0_ref[...], low_10_ref[...]
    upper_1, inv_1 = factor_tile(square_ref[...])
    inv_10 = -dot_full(inv_1, dot_full(low_10, inv_0))
    low_ref[:TILE, :TILE] = upper_ref[...].T
    low_ref[:TILE, TILE:] = zero
    low_ref[TILE:, :TILE] = low_10
    low_ref[TILE:, TILE:] = upper_1.T
    first = jnp.concatenate([inv_0, zero], axis=1)
    second = jnp.concatenate([inv_10, inv_1], axis=1)
    inv_ref[...] = spread_halves(jnp.concatenate([first, second], axis=0))
    first = jnp.concatenate([inv_0.T, inv_10.T], axis=1)
    second = jnp.concatenate([zero, inv_1.T], axis=1)
    stack_halves(inv_t_ref, jnp.concatenate([first, second], axis=0))


def factor_first(corner):
    tile = jax.ShapeDtypeStruct((TILE, TILE), jnp.float32)
    return pl.pallas_call(
        first_kernel,
        out_shape=(tile,) * 4,
        compiler_params=pltpu.CompilerParams(vmem_limit_bytes=VMEM_LIMIT),
        cost_estimate=pl.CostEstimate(flops=20_000_000, bytes_accessed=1 << 19, transcendentals=0),
    )(corner)


def factor_second(*parts):
    return pl.pallas_call(
        second_kernel,
        out_shape=(
            jax.ShapeDtypeStruct((WIDE, WIDE), jnp.float32),
            jax.ShapeDtypeStruct((WIDE, 3 * WIDE), jnp.bfloat16),
            jax.ShapeDtypeStruct((3 * WIDE, WIDE), jnp.bfloat16),
        ),
        compiler_params=pltpu.CompilerParams(vmem_limit_bytes=VMEM_LIMIT),
        cost_estimate=pl.CostEstimate(flops=20_000_000, bytes_accessed=1 << 20, transcendentals=0),
    )(*parts)


def columns_kernel(info_ref, inv_ref, *refs):
    out_ref, stack = refs[-2:]
    odd = info_ref[0] % 2 == 1
    start = 0
    for mine_ref, other_ref in zip(refs[0:-2:2], refs[1:-2:2]):
        size = mine_ref.shape[1]
        here = pl.ds(start, size)
        mine, other = mine_ref[...], other_ref[...]
        first = jnp.where(odd, other, mine)
        second = jnp.where(odd, mine, other)
        stack_halves(stack.at[:, here], jnp.concatenate([first, second], axis=0))
        stack_halves(out_ref.at[:, here], dot_half(inv_ref[...], stack[:, here]))
        start += size


def solve_columns(info, inverse, pairs):
    flat = [array for pair in pairs for array in pair]
    total = sum(pair[0].shape[1] for pair in pairs)
    vmem = pl.BlockSpec(memory_space=pltpu.VMEM)
    return pl.pallas_call(
        columns_kernel,
        in_specs=[pl.BlockSpec(memory_space=pltpu.SMEM)] + [vmem] * (1 + len(flat)),
        out_specs=vmem,
        out_shape=jax.ShapeDtypeStruct((3 * WIDE, total), jnp.bfloat16),
        scratch_shapes=[pltpu.VMEM((3 * WIDE, total), jnp.bfloat16)],
        compiler_params=pltpu.CompilerParams(vmem_limit_bytes=VMEM_LIMIT),
        cost_estimate=pl.CostEstimate(
            flops=6 * WIDE * WIDE * total, bytes_accessed=WIDE * total * 8, transcendentals=0
        ),
    )(info, inverse, *flat)


def update_kernel(
    start, block, info_ref, mat_ref, right_ref, lower_ref, inv_t_ref, mine_ref, other_ref, *refs
):
    out_ref, taken, given, panel, first_panel, in_sems, out_sems = refs[-7:]
    row, core, col = info_ref[0], info_ref[2], info_ref[3]
    rows, columns = mine_ref.shape[0], mat_ref.shape[1]
    steps = columns // block
    part = next(p for p in (512, 256, TILE) if rows % p == 0)
    piece = rows // PIECES

    def across(step):
        return pl.ds(pl.multiple_of(step * block, TILE), block)

    def take(step, slot):
        for p in range(PIECES):
            pltpu.make_async_copy(
                mat_ref.at[pl.ds(start + p * piece, piece), across(step)],
                taken.at[slot, pl.ds(p * piece, piece)],
                in_sems.at[slot],
            ).start()

    def give(step, slot):
        for p in range(PIECES):
            pltpu.make_async_copy(
                given.at[slot, pl.ds(p * piece, piece)],
                out_ref.at[pl.ds(start + p * piece, piece), across(step)],
                out_sems.at[slot],
            ).start()

    def wait_taken(step, slot):
        whole = mat_ref.at[pl.ds(start, rows), across(step)]
        pltpu.make_async_copy(whole, taken.at[slot], in_sems.at[slot]).wait()

    def wait_given(step, slot):
        whole = out_ref.at[pl.ds(start, rows), across(step)]
        pltpu.make_async_copy(given.at[slot], whole, out_sems.at[slot]).wait()

    for step in range(min(IN_SLOTS, steps)):
        take(step, step)

    @pl.loop(0, rows // part)
    def _(index):
        here = pl.ds(pl.multiple_of(index * part, part), part)
        mine, other = mine_ref[here], other_ref[here]
        raw = jnp.concatenate(
            [jnp.where(core == 1, other, mine), jnp.where(core == 1, mine, other)], axis=1
        )
        solved = dot_half(spread_halves(raw), inv_t_ref[...])
        panel[here] = spread_halves(solved)
        first_panel[here] = jnp.where(col == 1, solved[:, TILE:], solved[:, :TILE])

    if start == 0:

        @pl.when(row < PANELS)
        def _():
            head = jnp.where(row == 0, lower_ref[:TILE], lower_ref[TILE:])
            panel[:TILE] = spread_halves(head)
            first_panel[:TILE] = jnp.where(col == 1, head[:, TILE:], head[:, :TILE])

    @pl.loop(0, steps)
    def _(step):
        in_slot, out_slot = lax.rem(step, IN_SLOTS), lax.rem(step, OUT_SLOTS)
        wait_taken(step, in_slot)

        @pl.when(step >= OUT_SLOTS)
        def _():
            wait_given(step - OUT_SLOTS, out_slot)

        @pl.loop(0, rows // part)
        def _(index):
            here = pl.ds(pl.multiple_of(index * part, part), part)
            product = dot_half(panel[here], right_ref[:, across(step)])
            given[out_slot, here] = taken[in_slot, here] - product

        if start == 0:

            @pl.when(row < PANELS)
            def _():
                given[out_slot, :TILE] = jnp.zeros((TILE, block), jnp.float32)

        @pl.when(jnp.logical_and(step == 0, col < PANELS))
        def _():
            given[out_slot, :, :TILE] = first_panel[...]

        give(step, out_slot)

        @pl.when(step + IN_SLOTS < steps)
        def _():
            take(step + IN_SLOTS, in_slot)

    for step in range(max(steps - OUT_SLOTS, 0), steps):
        wait_given(step, step % OUT_SLOTS)


def update_rows(start, info, matrix, right, lower, inv_t, mine, other, out):
    rows, columns = mine.shape[0], matrix.shape[1]
    block = next(b for b in (512, 640, 256, TILE) if columns % b == 0)
    any_spec = pl.BlockSpec(memory_space=pl.ANY)
    vmem = pl.BlockSpec(memory_space=pltpu.VMEM)
    in_specs = [pl.BlockSpec(memory_space=pltpu.SMEM), any_spec] + [vmem] * 5
    operands = [info, matrix, right, lower, inv_t, mine, other]
    aliases = {}
    if out is not None:
        aliases = {len(operands): 0}
        in_specs.append(any_spec)
        operands.append(out)
    return pl.pallas_call(
        functools.partial(update_kernel, start, block),
        in_specs=in_specs,
        out_specs=any_spec,
        out_shape=jax.ShapeDtypeStruct(matrix.shape, jnp.float32),
        scratch_shapes=[
            pltpu.VMEM((IN_SLOTS, rows, block), jnp.float32),
            pltpu.VMEM((OUT_SLOTS, rows, block), jnp.float32),
            pltpu.VMEM((rows, 3 * WIDE), jnp.bfloat16),
            pltpu.VMEM((rows, TILE), jnp.float32),
            pltpu.SemaphoreType.DMA((IN_SLOTS,)),
            pltpu.SemaphoreType.DMA((OUT_SLOTS,)),
        ],
        input_output_aliases=aliases,
        compiler_params=pltpu.CompilerParams(vmem_limit_bytes=VMEM_LIMIT),
        cost_estimate=pl.CostEstimate(
            flops=6 * rows * columns * WIDE,
            bytes_accessed=8 * rows * columns,
            transcendentals=0,
        ),
    )(*operands)


def after(value, *earlier):
    return lax.optimization_barrier((value, *earlier))[0]


def double_rows(block, row, row_count, *earlier):
    stride = PANELS
    while stride < row_count:
        pairs = [(i, i + stride) for i in range(min(stride, row_count - stride))]
        got = after(lax.ppermute(block, "row", pairs), *earlier)
        block = jnp.where(jnp.logical_and(row >= stride, row < 2 * stride), got, block)
        stride *= 2
    return block


def swap_rows(block, row_count):
    return lax.ppermute(block, "row", [(i, i ^ 1) for i in range(row_count)])


def pick(blocks, index):
    chosen = blocks[0]
    for shift in range(1, len(blocks)):
        chosen = jnp.where(index == shift, blocks[shift], chosen)
    return chosen


def share_tile(tile, row, row_count, col_count):
    got = [tile]
    for shift in range(1, row_count):
        pairs = [
            (p * col_count + c, (p + shift) % row_count * col_count + c)
            for p in range(PANELS)
            for c in range(CORES)
        ]
        got.append(lax.ppermute(tile, ("row", "col"), pairs))
    return jnp.concatenate([pick(got, (row - p) % row_count) for p in range(PANELS)], axis=0)


def share_corner(column, earlier, place, core, col_count):
    got = [column]
    for shift in range(1, col_count // CORES):
        pairs = [(c, c + CORES * shift) for c in range(CORES)]
        got.append(lax.ppermute(column, "col", pairs))
    column = after(pick(got, place), earlier)
    beside = lax.ppermute(column, "col", [(c, c ^ 1) for c in range(col_count)])
    halves = [jnp.where(core == 0, column, beside), jnp.where(core == 0, beside, column)]
    return jnp.concatenate(halves, axis=1)


def per_device(matrix):
    row_count = lax.axis_size("row")
    col_count = lax.axis_size("col")
    row = lax.axis_index("row")
    col = lax.axis_index("col")
    depth = col_count // CORES
    place, core = col // CORES, col % CORES
    info = jnp.stack([row, place, core, col]).astype(jnp.int32)
    tiles = matrix.shape[0] // TILE
    chunks = next(n for n in (5, 4, 2, 1) if tiles % n == 0)
    rows = tiles // chunks * TILE
    half = matrix.shape[1] // 2
    swap = [(c, c ^ 1) for c in range(col_count)]

    last = chunks + depth - 2
    held, got = [], None

    def fill(*earlier):
        slot = len(held)
        if slot < chunks:
            own = matrix[slot * rows : (slot + 1) * rows, :TILE]
            block = own if got is None else jnp.where(place == 0, own, got)
        else:
            block = got
        held.append(after(block, *earlier))
        busy = [c for c in range(col_count) if 0 <= slot - c // CORES < chunks]
        hops = [(c, c + CORES) for c in busy if c + CORES < col_count]
        return lax.ppermute(held[-1], "col", hops) if slot < last else None

    ready = []

    def exchange(*earlier):
        chunk = len(ready)
        mine = after(pick(held[chunk : chunk + depth], place), *earlier)
        ready.append((mine, lax.ppermute(mine, "col", swap)))
        return mine

    got = fill()
    tile = after(matrix[:TILE, :TILE], held[0])
    column = after(share_tile(tile, row, row_count, col_count), got)
    got = fill(column)
    bands = [after(matrix[:TILE, :half], held[1]), after(matrix[:TILE, half:], held[1])]
    column = after(column, *bands)
    bands[0] = double_rows(bands[0], row, row_count)
    corner = share_corner(column, bands[0], place, core, col_count)
    got = fill()
    parts = factor_first(after(corner, held[2]))
    while len(held) < depth:
        got = fill(parts[3])
    bands[1] = double_rows(bands[1], row, row_count, parts[3])
    besides = [swap_rows(band, row_count) for band in bands]
    mark = exchange()
    square = after(parts[3], held[-1], mark, bands[1])
    lower, inverse, inv_t = factor_second(*parts[:3], square)
    got = fill(inverse, besides[0])
    mark = exchange()
    right = solve_columns(info, after(inverse, held[-1]), list(zip(bands, besides)))
    out = None
    for chunk in range(chunks):
        mine, other = ready[chunk]
        other = after(other, held[-1], mark)
        out = update_rows(chunk * rows, info, matrix, right, lower, inv_t, mine, other, out)
        if len(held) <= last:
            got = fill(mark, out)
            mark = exchange(out)
    return out


def solution(mesh):
    return jax.shard_map(
        per_device,
        mesh=mesh,
        in_specs=(P("row", "col"),),
        out_specs=P("row", "col"),
        check_vma=False,
    )
```

```python
import functools

import jax
import jax.numpy as jnp
from jax import lax
from jax.experimental import pallas as pl
from jax.experimental.pallas import tpu as pltpu
from jax.sharding import PartitionSpec as P

TILE = 128
PANELS = 2
WIDE = PANELS * TILE
CORES = 2
VMEM_LIMIT = 40 * 1024 * 1024
GROUP = 8
IN_SLOTS = 4
OUT_SLOTS = 3
PIECES = 4


def dot_full(left, right, dims=((1,), (0,))):
    return lax.dot_general(
        left,
        right,
        (dims, ((), ())),
        precision=lax.Precision.HIGHEST,
        preferred_element_type=jnp.float32,
    )


def dot_half(left, right):
    return lax.dot_general(
        left, right, (((1,), (0,)), ((), ())), preferred_element_type=jnp.float32
    )


def split_half(value):
    high = value.astype(jnp.bfloat16)
    low = (value - high.astype(jnp.float32)).astype(jnp.bfloat16)
    return high, low


def stack_halves(ref, value):
    high, low = split_half(value)
    ref[:WIDE] = high
    ref[WIDE : 2 * WIDE] = low
    ref[2 * WIDE :] = high


def spread_halves(value):
    high, low = split_half(value)
    return jnp.concatenate([high, high, low], axis=1)


def factor_tile(square):
    groups = TILE // GROUP
    shape = (GROUP, TILE)
    lane = lax.broadcasted_iota(jnp.int32, shape, 1)
    sub = lax.broadcasted_iota(jnp.int32, shape, 0)
    left = [square[g * GROUP : (g + 1) * GROUP] for g in range(groups)]
    right = [jnp.where(lane == sub + g * GROUP, 1.0, 0.0) for g in range(groups)]

    def row_of(value, index):
        return jnp.broadcast_to(value[index : index + 1], shape)

    def column_of(value, index):
        return jnp.broadcast_to(value[:, index : index + 1], shape)

    for g in range(groups):
        first = g * GROUP
        span = range(GROUP)
        columns = [column_of(left[g], first + b) for b in span]
        block = [[row_of(columns[b], a) if a <= b else None for b in span] for a in span]
        ratio = [[None] * GROUP for _ in span]
        inverse = []
        for s in span:
            inverse.append(1.0 / block[s][s])
            for t in range(s + 1, GROUP):
                ratio[t][s] = block[s][t] * inverse[s]
            for t in range(s + 1, GROUP):
                for b in range(t, GROUP):
                    block[t][b] = block[t][b] - ratio[t][s] * block[s][b]
        rows_left = [row_of(left[g], s) for s in span]
        rows_right = [row_of(right[g], s) for s in span]
        for t in span:
            for s in range(t):
                rows_left[t] = rows_left[t] - ratio[t][s] * rows_left[s]
                rows_right[t] = rows_right[t] - ratio[t][s] * rows_right[s]
        for s in span:
            left[g] = jnp.where(sub == s, rows_left[s], left[g])
            right[g] = jnp.where(sub == s, rows_right[s], right[g])
        rows_left = [rows_left[s] * inverse[s] for s in span]
        rows_right = [rows_right[s] * inverse[s] for s in span]
        for other in range(g + 1, groups):
            columns = [column_of(left[other], first + s) for s in span]
            for s in span:
                for t in range(s):
                    columns[s] = columns[s] - ratio[s][t] * columns[t]
            for s in span:
                left[other] = left[other] - columns[s] * rows_left[s]
                right[other] = right[other] - columns[s] * rows_right[s]
    upper, inverse = [], []
    for g in range(groups):
        row = sub + g * GROUP
        pivot = jnp.sum(jnp.where(lane == row, left[g], 0.0), axis=1, keepdims=True)
        scale = 1.0 / jnp.sqrt(pivot)
        upper.append(jnp.where(lane >= row, left[g] * scale, 0.0))
        inverse.append(right[g] * scale)
    return jnp.concatenate(upper, axis=0), jnp.concatenate(inverse, axis=0)


def first_kernel(corner_ref, upper_ref, inv_ref, low_ref, square_ref):
    upper, inverse = factor_tile(corner_ref[:TILE, :TILE])
    low = dot_full(corner_ref[TILE:, :TILE], inverse, ((1,), (1,)))
    upper_ref[...] = upper
    inv_ref[...] = inverse
    low_ref[...] = low
    square_ref[...] = corner_ref[TILE:, TILE:] - dot_full(low, low, ((1,), (1,)))


def second_kernel(upper_ref, inv_0_ref, low_10_ref, square_ref, low_ref, inv_ref, inv_t_ref):
    zero = jnp.zeros((TILE, TILE), jnp.float32)
    inv_0, low_10 = inv_0_ref[...], low_10_ref[...]
    upper_1, inv_1 = factor_tile(square_ref[...])
    inv_10 = -dot_full(inv_1, dot_full(low_10, inv_0))
    low_ref[:TILE, :TILE] = upper_ref[...].T
    low_ref[:TILE, TILE:] = zero
    low_ref[TILE:, :TILE] = low_10
    low_ref[TILE:, TILE:] = upper_1.T
    first = jnp.concatenate([inv_0, zero], axis=1)
    second = jnp.concatenate([inv_10, inv_1], axis=1)
    inv_ref[...] = spread_halves(jnp.concatenate([first, second], axis=0))
    first = jnp.concatenate([inv_0.T, inv_10.T], axis=1)
    second = jnp.concatenate([zero, inv_1.T], axis=1)
    stack_halves(inv_t_ref, jnp.concatenate([first, second], axis=0))


def factor_first(corner):
    tile = jax.ShapeDtypeStruct((TILE, TILE), jnp.float32)
    return pl.pallas_call(
        first_kernel,
        out_shape=(tile,) * 4,
        compiler_params=pltpu.CompilerParams(vmem_limit_bytes=VMEM_LIMIT),
        cost_estimate=pl.CostEstimate(flops=20_000_000, bytes_accessed=1 << 19, transcendentals=0),
    )(corner)


def factor_second(*parts):
    return pl.pallas_call(
        second_kernel,
        out_shape=(
            jax.ShapeDtypeStruct((WIDE, WIDE), jnp.float32),
            jax.ShapeDtypeStruct((WIDE, 3 * WIDE), jnp.bfloat16),
            jax.ShapeDtypeStruct((3 * WIDE, WIDE), jnp.bfloat16),
        ),
        compiler_params=pltpu.CompilerParams(vmem_limit_bytes=VMEM_LIMIT),
        cost_estimate=pl.CostEstimate(flops=20_000_000, bytes_accessed=1 << 20, transcendentals=0),
    )(*parts)


def columns_kernel(info_ref, inv_ref, *refs):
    out_ref, stack = refs[-2:]
    odd = info_ref[0] % 2 == 1
    start = 0
    for mine_ref, other_ref in zip(refs[0:-2:2], refs[1:-2:2]):
        size = mine_ref.shape[1]
        here = pl.ds(start, size)
        mine, other = mine_ref[...], other_ref[...]
        first = jnp.where(odd, other, mine)
        second = jnp.where(odd, mine, other)
        stack_halves(stack.at[:, here], jnp.concatenate([first, second], axis=0))
        stack_halves(out_ref.at[:, here], dot_half(inv_ref[...], stack[:, here]))
        start += size


def solve_columns(info, inverse, pairs):
    flat = [array for pair in pairs for array in pair]
    total = sum(pair[0].shape[1] for pair in pairs)
    vmem = pl.BlockSpec(memory_space=pltpu.VMEM)
    return pl.pallas_call(
        columns_kernel,
        in_specs=[pl.BlockSpec(memory_space=pltpu.SMEM)] + [vmem] * (1 + len(flat)),
        out_specs=vmem,
        out_shape=jax.ShapeDtypeStruct((3 * WIDE, total), jnp.bfloat16),
        scratch_shapes=[pltpu.VMEM((3 * WIDE, total), jnp.bfloat16)],
        compiler_params=pltpu.CompilerParams(vmem_limit_bytes=VMEM_LIMIT),
        cost_estimate=pl.CostEstimate(
            flops=6 * WIDE * WIDE * total, bytes_accessed=WIDE * total * 8, transcendentals=0
        ),
    )(info, inverse, *flat)


def update_kernel(
    start, block, info_ref, mat_ref, right_ref, lower_ref, inv_t_ref, mine_ref, other_ref, *refs
):
    out_ref, taken, given, panel, first_panel, in_sems, out_sems = refs[-7:]
    row, core, col = info_ref[0], info_ref[2], info_ref[3]
    rows, columns = mine_ref.shape[0], mat_ref.shape[1]
    steps = columns // block
    part = next(p for p in (512, 256, TILE) if rows % p == 0)
    piece = rows // PIECES

    def across(step):
        return pl.ds(pl.multiple_of(step * block, TILE), block)

    def take(step, slot):
        for p in range(PIECES):
            pltpu.make_async_copy(
                mat_ref.at[pl.ds(start + p * piece, piece), across(step)],
                taken.at[slot, pl.ds(p * piece, piece)],
                in_sems.at[slot],
            ).start()

    def give(step, slot):
        for p in range(PIECES):
            pltpu.make_async_copy(
                given.at[slot, pl.ds(p * piece, piece)],
                out_ref.at[pl.ds(start + p * piece, piece), across(step)],
                out_sems.at[slot],
            ).start()

    def wait_taken(step, slot):
        whole = mat_ref.at[pl.ds(start, rows), across(step)]
        pltpu.make_async_copy(whole, taken.at[slot], in_sems.at[slot]).wait()

    def wait_given(step, slot):
        whole = out_ref.at[pl.ds(start, rows), across(step)]
        pltpu.make_async_copy(given.at[slot], whole, out_sems.at[slot]).wait()

    for step in range(min(IN_SLOTS, steps)):
        take(step, step)

    @pl.loop(0, rows // part)
    def _(index):
        here = pl.ds(pl.multiple_of(index * part, part), part)
        mine, other = mine_ref[here], other_ref[here]
        raw = jnp.concatenate(
            [jnp.where(core == 1, other, mine), jnp.where(core == 1, mine, other)], axis=1
        )
        solved = dot_half(spread_halves(raw), inv_t_ref[...])
        panel[here] = spread_halves(solved)
        first_panel[here] = jnp.where(col == 1, solved[:, TILE:], solved[:, :TILE])

    if start == 0:

        @pl.when(row < PANELS)
        def _():
            head = jnp.where(row == 0, lower_ref[:TILE], lower_ref[TILE:])
            panel[:TILE] = spread_halves(head)
            first_panel[:TILE] = jnp.where(col == 1, head[:, TILE:], head[:, :TILE])

    @pl.loop(0, steps)
    def _(step):
        in_slot, out_slot = lax.rem(step, IN_SLOTS), lax.rem(step, OUT_SLOTS)
        wait_taken(step, in_slot)

        @pl.when(step >= OUT_SLOTS)
        def _():
            wait_given(step - OUT_SLOTS, out_slot)

        @pl.loop(0, rows // part)
        def _(index):
            here = pl.ds(pl.multiple_of(index * part, part), part)
            product = dot_half(panel[here], right_ref[:, across(step)])
            given[out_slot, here] = taken[in_slot, here] - product

        if start == 0:

            @pl.when(row < PANELS)
            def _():
                given[out_slot, :TILE] = jnp.zeros((TILE, block), jnp.float32)

        @pl.when(jnp.logical_and(step == 0, col < PANELS))
        def _():
            given[out_slot, :, :TILE] = first_panel[...]

        give(step, out_slot)

        @pl.when(step + IN_SLOTS < steps)
        def _():
            take(step + IN_SLOTS, in_slot)

    for step in range(max(steps - OUT_SLOTS, 0), steps):
        wait_given(step, step % OUT_SLOTS)


def update_rows(start, info, matrix, right, lower, inv_t, mine, other, out):
    rows, columns = mine.shape[0], matrix.shape[1]
    block = next(b for b in (512, 640, 256, TILE) if columns % b == 0)
    any_spec = pl.BlockSpec(memory_space=pl.ANY)
    vmem = pl.BlockSpec(memory_space=pltpu.VMEM)
    in_specs = [pl.BlockSpec(memory_space=pltpu.SMEM), any_spec] + [vmem] * 5
    operands = [info, matrix, right, lower, inv_t, mine, other]
    aliases = {}
    if out is not None:
        aliases = {len(operands): 0}
        in_specs.append(any_spec)
        operands.append(out)
    return pl.pallas_call(
        functools.partial(update_kernel, start, block),
        in_specs=in_specs,
        out_specs=any_spec,
        out_shape=jax.ShapeDtypeStruct(matrix.shape, jnp.float32),
        scratch_shapes=[
            pltpu.VMEM((IN_SLOTS, rows, block), jnp.float32),
            pltpu.VMEM((OUT_SLOTS, rows, block), jnp.float32),
            pltpu.VMEM((rows, 3 * WIDE), jnp.bfloat16),
            pltpu.VMEM((rows, TILE), jnp.float32),
            pltpu.SemaphoreType.DMA((IN_SLOTS,)),
            pltpu.SemaphoreType.DMA((OUT_SLOTS,)),
        ],
        input_output_aliases=aliases,
        compiler_params=pltpu.CompilerParams(vmem_limit_bytes=VMEM_LIMIT),
        cost_estimate=pl.CostEstimate(
            flops=6 * rows * columns * WIDE,
            bytes_accessed=8 * rows * columns,
            transcendentals=0,
        ),
    )(*operands)


def after(value, *earlier):
    return lax.optimization_barrier((value, *earlier))[0]


def double_rows(block, row, row_count, *earlier):
    stride = PANELS
    while stride < row_count:
        pairs = [(i, i + stride) for i in range(min(stride, row_count - stride))]
        got = after(lax.ppermute(block, "row", pairs), *earlier)
        block = jnp.where(jnp.logical_and(row >= stride, row < 2 * stride), got, block)
        stride *= 2
    return block


def swap_rows(block, row_count):
    return lax.ppermute(block, "row", [(i, i ^ 1) for i in range(row_count)])


def pick(blocks, index):
    chosen = blocks[0]
    for shift in range(1, len(blocks)):
        chosen = jnp.where(index == shift, blocks[shift], chosen)
    return chosen


def share_tile(tile, row, row_count, col_count):
    got = [tile]
    for shift in range(1, row_count):
        pairs = [
            (p * col_count + c, (p + shift) % row_count * col_count + c)
            for p in range(PANELS)
            for c in range(CORES)
        ]
        got.append(lax.ppermute(tile, ("row", "col"), pairs))
    return jnp.concatenate([pick(got, (row - p) % row_count) for p in range(PANELS)], axis=0)


def share_corner(column, earlier, place, core, col_count):
    got = [column]
    for shift in range(1, col_count // CORES):
        pairs = [(c, c + CORES * shift) for c in range(CORES)]
        got.append(lax.ppermute(column, "col", pairs))
    column = after(pick(got, place), earlier)
    beside = lax.ppermute(column, "col", [(c, c ^ 1) for c in range(col_count)])
    halves = [jnp.where(core == 0, column, beside), jnp.where(core == 0, beside, column)]
    return jnp.concatenate(halves, axis=1)


def per_device(matrix):
    row_count = lax.axis_size("row")
    col_count = lax.axis_size("col")
    row = lax.axis_index("row")
    col = lax.axis_index("col")
    depth = col_count // CORES
    place, core = col // CORES, col % CORES
    info = jnp.stack([row, place, core, col]).astype(jnp.int32)
    tiles = matrix.shape[0] // TILE
    chunks = next(n for n in (5, 4, 2, 1) if tiles % n == 0)
    rows = tiles // chunks * TILE
    half = matrix.shape[1] // 2
    swap = [(c, c ^ 1) for c in range(col_count)]

    last = chunks + depth - 2
    held, got = [], None

    def fill(*earlier):
        slot = len(held)
        if slot < chunks:
            own = matrix[slot * rows : (slot + 1) * rows, :TILE]
            block = own if got is None else jnp.where(place == 0, own, got)
        else:
            block = got
        held.append(after(block, *earlier))
        busy = [c for c in range(col_count) if 0 <= slot - c // CORES < chunks]
        hops = [(c, c + CORES) for c in busy if c + CORES < col_count]
        return lax.ppermute(held[-1], "col", hops) if slot < last else None

    ready = []

    def exchange(*earlier):
        chunk = len(ready)
        mine = after(pick(held[chunk : chunk + depth], place), *earlier)
        ready.append((mine, lax.ppermute(mine, "col", swap)))
        return mine

    got = fill()
    tile = after(matrix[:TILE, :TILE], held[0])
    column = after(share_tile(tile, row, row_count, col_count), got)
    got = fill(column)
    bands = [after(matrix[:TILE, :half], held[1]), after(matrix[:TILE, half:], held[1])]
    column = after(column, *bands)
    bands[0] = double_rows(bands[0], row, row_count)
    corner = share_corner(column, bands[0], place, core, col_count)
    got = fill()
    parts = factor_first(after(corner, held[2]))
    while len(held) < depth:
        got = fill(parts[3])
    bands[1] = double_rows(bands[1], row, row_count, parts[3])
    besides = [swap_rows(band, row_count) for band in bands]
    mark = exchange()
    square = after(parts[3], held[-1], mark, bands[1])
    lower, inverse, inv_t = factor_second(*parts[:3], square)
    got = fill(inverse, besides[0])
    mark = exchange()
    right = solve_columns(info, after(inverse, held[-1]), list(zip(bands, besides)))
    out = None
    for chunk in range(chunks):
        mine, other = ready[chunk]
        other = after(other, held[-1], mark)
        out = update_rows(chunk * rows, info, matrix, right, lower, inv_t, mine, other, out)
        if len(held) <= last:
            got = fill(mark, out)
            mark = exchange(out)
    return out


def solution(mesh):
    return jax.shard_map(
        per_device,
        mesh=mesh,
        in_specs=(P("row", "col"),),
        out_specs=P("row", "col"),
        check_vma=False,
    )
```
